256 devices in a mesh: dp: 32 (over x_lo, z, core), tp: 8 (over x_hi, y).
Axes of the slice: x: 4 (x_hi: 2, x_lo: 2; x = x_hi * 2 + x_lo), y: 4, z: 8, core: 2. Of those that a mesh axis runs over, the one named last changes fastest.
Arguments:
- queries: bfloat16 [128, 3, 128, 576], P('dp', None, 'tp'), may hold values from -200 to 200
- new_latent: bfloat16 [128, 3, 576], P('dp'), may hold values from -6 to 6
- cache: bfloat16 [131072, 576], P('dp'), may hold values from -6 to 6
- cache_lengths: int32 [32, 4], replicated, may hold values from 1 to 2048, as said below
- w_uv: bfloat16 [128, 512, 128], P('tp'), may hold values from -1 to 1
- w_o: bfloat16 [16384, 7168], P('tp', 'dp'), may hold values from -0.09375 to 0.09375
- residual: bfloat16 [384, 7168], P(None, ('dp', 'tp')), may hold values from -6 to 6
- norm_gain: bfloat16 [7168], replicated, may hold values from 0.099609375 to 1.8984375
- w_gate: bfloat16 [7168, 18432], P(None, ('dp', 'tp')), may hold values from -0.3125 to 0.3125
- w_up: bfloat16 [7168, 18432], P(None, ('dp', 'tp')), may hold values from -0.3125 to 0.3125
- w_down: bfloat16 [18432, 7168], P(('dp', 'tp')), may hold values from -0.1875 to 0.1875
Outputs:
- layer_out: bfloat16 [384, 7168], P(None, ('dp', 'tp'))
The draws below stay inside these ranges and needn't reach their ends.
Inputs may be any that keep to these rules, and one draw needn't show every extreme that they name: `cache_lengths`: row d lists the cache lengths of the 4 requests of dp index d, packed in order from the first of that index's 4096 cache rows; every row sums to at most 4096; one request holds at most 4096 // min(4, 2) tokens, and some request holds exactly that many.
All inputs are finite; a program needn't handle non-finite values.
Results may differ from the reference program's by a relative error of at most 0.02.
Values may be sent and summed in bfloat16 or wider, within the bound.
No kernel may reach another device: no remote copies, remote signals or barrier semaphores. Data moves between devices by JAX's collectives and lax.ppermute only.
A program may use at most 128 MiB of HBM per device.

```python
import jax
import jax.numpy as jnp
from jax import lax

D = 7168
FF = 18432
HEADS = 128
LAT = 512
VDIM = 128
REQ_DEV = 4
CTX_DEV = 4096
STEPS = 3
KDIM = 576
TOKENS = 384
N_DP = 32


def base_lengths(key):
    key = jax.random.fold_in(key, 101)
    first_key, second_key, third_key = jax.random.split(key, 3)
    weight = jax.random.randint(first_key, (N_DP,), 1, 14)
    busiest = jax.random.randint(second_key, (), 0, N_DP)
    filled = (CTX_DEV * weight // 21).astype(jnp.int32)
    bound = CTX_DEV // min(REQ_DEV, 2)
    shares = jax.random.randint(third_key, (N_DP, REQ_DEV), 1, 9).astype(jnp.int32)
    share_total = jnp.sum(shares, axis=1, keepdims=True)
    general = 1 + (filled[:, None] - REQ_DEV) * shares // share_total
    general = jnp.minimum(general, bound)
    rest = CTX_DEV - bound
    later_shares = shares[:, 1:]
    later_total = jnp.maximum(jnp.sum(later_shares, axis=1, keepdims=True), 1)
    later = 1 + (rest - (REQ_DEV - 1)) * later_shares // later_total
    busy_row = jnp.concatenate([jnp.full((N_DP, 1), bound, jnp.int32), later.astype(jnp.int32)], axis=1)
    is_busy = (jnp.arange(N_DP) == busiest)[:, None]
    return jnp.where(is_busy, busy_row, general).astype(jnp.int32)


def base_cache(key):
    key = jax.random.fold_in(key, 202)
    return jnp.clip(jax.random.normal(key, (N_DP * CTX_DEV, KDIM), jnp.float32), -6.0, 6.0)


def draw_cache_lengths(key, part):
    return base_lengths(key)


def draw_cache(key, part):
    return base_cache(key).astype(jnp.bfloat16)


def draw_queries(key, part):
    own_key = jax.random.fold_in(key, 303)
    values = jnp.clip(jax.random.normal(own_key, (N_DP * REQ_DEV, STEPS, HEADS, KDIM), jnp.float32), -6.0, 6.0)
    return values.astype(jnp.bfloat16)


def raised(drawn, rng, source, target, shards_of, factor):
    owner, partner = [(jnp.arange(drawn.shape[dim]) // (drawn.shape[dim] // shards_of)).reshape([-1 if axis == dim else 1 for axis in range(drawn.ndim)]) for dim in (source, target)]
    chosen = jax.random.permutation(rng, shards_of)[partner]
    strong = (owner == chosen) | (owner == (partner + shards_of // 2) % shards_of)
    return jnp.where(strong, factor * drawn, drawn)


def levels(stream_key, dims, cuts, least, high):
    gain, own = 1.0, jax.random.fold_in(stream_key, 6)
    for axis_at, blocks in cuts:
        heights = jnp.exp(jax.random.uniform(jax.random.fold_in(own, axis_at), (blocks,), jnp.float32, least / len(cuts), high / len(cuts)))
        gain = gain * jnp.repeat(heights, dims[axis_at] // blocks).reshape([-1 if axis == axis_at else 1 for axis in range(len(dims))])
    return gain


def normal_values(stream_key, extent, width, most, shards=(), held_as=jnp.bfloat16):
    entries = jax.random.normal(stream_key, extent, jnp.float32) * width
    if len(shards) > 0:
        entries = levels(stream_key, extent, shards, -0.22, 0.18) * entries
    return jnp.clip(entries, min=-most, max=most).astype(held_as)


def bell_draw_with(key, dims, deviation, reach, shards, heavy, kind=jnp.bfloat16):
    drawn = deviation * jax.random.normal(key, dims, jnp.float32)
    if shards:
        drawn = drawn * levels(key, dims, shards, -0.22, 0.18)
    return jnp.clip(raised(drawn, jax.random.fold_in(key, 3), *heavy), -reach, reach).astype(kind)


def setup_inputs(seed: int = 0) -> dict:
    arg_keys = jax.random.split(jax.random.key(seed), 12)
    return {
        "queries": draw_queries(jax.random.fold_in(arg_keys[11], 71), 0),
        "new_latent": normal_values(arg_keys[1], (N_DP * REQ_DEV, STEPS, KDIM), 1.0, 6.0, ((0, 32),)),
        "cache": draw_cache(jax.random.fold_in(arg_keys[11], 71), 0),
        "cache_lengths": draw_cache_lengths(jax.random.fold_in(arg_keys[11], 71), 0),
        "w_uv": normal_values(arg_keys[4], (HEADS, LAT, VDIM), (LAT // 16) ** -0.5, 1.0, ((0, 8),)),
        "w_o": bell_draw_with(arg_keys[5], (HEADS * VDIM, D), (HEADS * VDIM) ** -0.5, 0.09375, ((0, 8), (1, 32)), (0, 1, 32, 2.75)),
        "residual": normal_values(arg_keys[6], (TOKENS, D), 1.0, 6.0, ((1, 256),)),
        "norm_gain": jnp.clip(1.0 + 0.18 * jax.random.normal(arg_keys[7], (D,), jnp.float32), 0.099609375, 1.8984375).astype(jnp.bfloat16),
        "w_gate": bell_draw_with(arg_keys[8], (D, FF), D ** -0.5, 0.3125, ((1, 256),), (0, 1, 256, 6.0)),
        "w_up": bell_draw_with(arg_keys[9], (D, FF), D ** -0.5, 0.3125, ((1, 256),), (0, 1, 256, 6.0)),
        "w_down": bell_draw_with(arg_keys[10], (FF, D), FF ** -0.5, 0.1875, ((0, 256),), (0, 1, 256, 6.0)),
    }


score_scale = 192.0 ** (-0.5)
big_negative = -1e+30

def device_attention(inputs, w_uv):
    queries_dev, fresh_dev, cache_dev, lengths_row = inputs
    starts = jnp.cumsum(lengths_row) - lengths_row
    filled = jnp.sum(lengths_row)
    slot_ids = jnp.arange(CTX_DEV, dtype=jnp.int32)
    labels = lax.optimization_barrier(jnp.sum((slot_ids[:, None] >= starts[None, :]).astype(jnp.int32), axis=1)) - 1
    labels = jnp.where(slot_ids < filled, labels, -1)
    query_wide = queries_dev.astype(jnp.float32)
    cache_wide = cache_dev.astype(jnp.float32)
    fresh_wide = fresh_dev.astype(jnp.float32)
    cache_scores = jnp.einsum('rthk,ck->rthc', query_wide, cache_wide) * score_scale
    fresh_scores = jnp.einsum('rthk,rsk->rths', query_wide, fresh_wide) * score_scale
    request_ids = jnp.arange(REQ_DEV, dtype=jnp.int32)
    allowed = labels[None, None, None, :] == request_ids[:, None, None, None]
    step_ids = jnp.arange(STEPS, dtype=jnp.int32)
    causal = (step_ids[None, :] <= step_ids[:, None])[None, :, None, :]
    row_max = jnp.maximum(lax.optimization_barrier(jnp.max(jnp.where(allowed, cache_scores, big_negative), axis=-1)), lax.optimization_barrier(jnp.max(jnp.where(causal, fresh_scores, big_negative), axis=-1)))
    cache_weights = jnp.where(allowed, jnp.exp(cache_scores - row_max[..., None]), 0.0)
    fresh_weights = jnp.where(causal, jnp.exp(fresh_scores - row_max[..., None]), 0.0)
    denominators = lax.optimization_barrier(jnp.sum(cache_weights, axis=-1)) + lax.optimization_barrier(jnp.sum(fresh_weights, axis=-1))
    cache_rounded = lax.optimization_barrier(cache_weights.astype(jnp.bfloat16)).astype(jnp.float32)
    fresh_rounded = lax.optimization_barrier(fresh_weights.astype(jnp.bfloat16)).astype(jnp.float32)
    weighted = jnp.einsum('rthc,cl->rthl', cache_rounded, cache_wide[:, :LAT])
    weighted = weighted + jnp.einsum('rths,rsl->rthl', fresh_rounded, fresh_wide[..., :LAT])
    mixed_latent = (weighted / denominators[..., None]).astype(jnp.bfloat16)
    mixed_wide = lax.optimization_barrier(mixed_latent).astype(jnp.float32)
    head_values = jnp.einsum('rthl,hlv->rthv', mixed_wide, w_uv.astype(jnp.float32))
    return head_values.astype(jnp.bfloat16).reshape(REQ_DEV * STEPS, HEADS * VDIM)

def reference(queries, new_latent, cache, cache_lengths, w_uv, w_o, residual, norm_gain, w_gate, w_up, w_down):
    stacked = (queries.reshape(N_DP, REQ_DEV, STEPS, HEADS, KDIM), new_latent.reshape(N_DP, REQ_DEV, STEPS, KDIM), cache.reshape(N_DP, CTX_DEV, KDIM), cache_lengths)
    head_values = lax.map(lambda item: device_attention(item, w_uv), stacked)
    head_values = head_values.reshape(TOKENS, HEADS * VDIM)
    attended = jnp.dot(head_values, w_o, preferred_element_type=jnp.float32)
    updated = (residual.astype(jnp.float32) + attended).astype(jnp.bfloat16)
    widened = updated.astype(jnp.float32)
    inverse_rms = lax.rsqrt(lax.optimization_barrier(jnp.mean(widened * widened, axis=-1, keepdims=True)) + 1e-06)
    normed = (widened * inverse_rms * norm_gain.astype(jnp.float32)).astype(jnp.bfloat16)
    gate_out = jnp.dot(normed, w_gate, preferred_element_type=jnp.float32)
    up_out = jnp.dot(normed, w_up, preferred_element_type=jnp.float32)
    hidden = (jax.nn.silu(gate_out) * up_out).astype(jnp.bfloat16)
    ffn_sum = jnp.dot(hidden, w_down, preferred_element_type=jnp.float32)
    return (updated.astype(jnp.float32) + ffn_sum).astype(jnp.bfloat16)
```

```python
import functools

import jax
import jax.numpy as jnp
import numpy as np
from jax import lax
from jax.experimental import pallas as pl
from jax.experimental.pallas import tpu as pltpu
from jax.sharding import Mesh, PartitionSpec as P

DP = ("xl", "z", "c")
RING = ("xl", "z")
TP = ("xh", "y")
SIZES = {"xl": 2, "z": 8, "c": 2, "xh": 2, "y": 4}
N_RING, N_TP = 16, 8

STEPS, HEADS, REQ = 3, 16, 4
NEW = REQ * STEPS
ROWS = NEW * HEADS
TOKENS = 384
LAT, KDIM, VDIM = 512, 576, 128
CTX, CHUNK = 4096, 512
N_CHUNK = CTX // CHUNK
D, FEAT, PIECE, PAD = 7168, 224, 28, 32
FF = 72
EPS = 1e-06
LOG2E = 1.4426950408889634
SCALE = 192.0 ** (-0.5)
NEG = -1e30

NT = (((1,), (1,)), ((), ()))
TN = (((0,), (0,)), ((), ()))


def dot(a, b, dims=(((1,), (0,)), ((), ()))):
    return lax.dot_general(a, b, dims, preferred_element_type=jnp.float32)


def attend_kernel(
    bounds, q_ref, fresh_ref, cache_hbm, w_uv_hbm, out_ref, keys, scores, w_uv, key_sems, w_sem
):
    copies = [
        pltpu.make_async_copy(
            cache_hbm.at[:, pl.ds(j * CHUNK, CHUNK)], keys.at[j], key_sems.at[j]
        )
        for j in range(N_CHUNK)
    ]
    w_copy = pltpu.make_async_copy(w_uv_hbm, w_uv, w_sem)
    for copy in copies:
        copy.start()
    w_copy.start()

    q = q_ref[...]
    row = lax.broadcasted_iota(jnp.int32, (ROWS, 1), 0)
    request = row // (STEPS * HEADS)
    step = row // HEADS - request * STEPS
    low = jnp.zeros((ROWS, 1), jnp.int32)
    high = jnp.zeros((ROWS, 1), jnp.int32)
    for r in range(REQ):
        low = jnp.where(request == r, bounds[r], low)
        high = jnp.where(request == r, bounds[REQ + r], high)

    fresh = fresh_ref[...]
    key = lax.broadcasted_iota(jnp.int32, (ROWS, NEW), 1)
    key_step = key // REQ
    seen = (key - key_step * REQ == request) & (key_step <= step)
    fresh_scores = jnp.where(seen, dot(q, fresh, NT) * (SCALE * LOG2E), NEG)
    top = jnp.max(fresh_scores, axis=1, keepdims=True)

    for j in range(N_CHUNK):
        copies[j].wait()
        slot = j * CHUNK + lax.broadcasted_iota(jnp.int32, (ROWS, CHUNK), 1)
        part = dot(q, keys[j]) * (SCALE * LOG2E)
        part = jnp.where((slot >= low) & (slot < high), part, NEG)
        scores[j] = part
        top = jnp.maximum(top, jnp.max(part, axis=1, keepdims=True))

    weights = jnp.exp2(fresh_scores - top)
    total = jnp.sum(weights, axis=1, keepdims=True)
    mixed = dot(weights.astype(jnp.bfloat16), fresh[:, :LAT])
    for j in range(N_CHUNK):
        weights = jnp.exp2(scores[j] - top)
        total = total + jnp.sum(weights, axis=1, keepdims=True)
        mixed = mixed + dot(weights.astype(jnp.bfloat16), keys[j, :LAT, :], NT)
    mixed = (mixed / total).astype(jnp.bfloat16)

    w_copy.wait()
    head = row - (row // HEADS) * HEADS
    for h in range(HEADS):
        values = jnp.where(head == h, dot(mixed, w_uv[h]), 0.0)
        values = jnp.sum(values.reshape(NEW, HEADS, VDIM), axis=1).astype(jnp.bfloat16)
        half, at = h // (HEADS // 2), h % (HEADS // 2)
        out_ref[half, :, at * VDIM : (at + 1) * VDIM] = values


def attend(bounds, q, fresh, cache_t, w_uv):
    vmem = pl.BlockSpec(memory_space=pltpu.VMEM)
    anyspace = pl.BlockSpec(memory_space=pl.ANY)
    return pl.pallas_call(
        attend_kernel,
        out_shape=jax.ShapeDtypeStruct((2, NEW, HEADS // 2 * VDIM), jnp.bfloat16),
        in_specs=[
            pl.BlockSpec(memory_space=pltpu.SMEM),
            vmem,
            vmem,
            anyspace,
            anyspace,
        ],
        out_specs=vmem,
        scratch_shapes=[
            pltpu.VMEM((N_CHUNK, KDIM, CHUNK), jnp.bfloat16),
            pltpu.VMEM((N_CHUNK, ROWS, CHUNK), jnp.float32),
            pltpu.VMEM((HEADS, LAT, VDIM), jnp.bfloat16),
            pltpu.SemaphoreType.DMA((N_CHUNK,)),
            pltpu.SemaphoreType.DMA,
        ],
        compiler_params=pltpu.CompilerParams(vmem_limit_bytes=40 * 2**20),
        cost_estimate=pl.CostEstimate(
            flops=2 * ROWS * CTX * (KDIM + LAT), bytes_accessed=7 * 2**20, transcendentals=ROWS * CTX
        ),
        name="attend",
    )(bounds, q, fresh, cache_t, w_uv)


def regroup_kernel(source_ref, gate_ref, up_ref, down_ref, mix_ref, out_ref):
    width = 4 * FEAT
    lanes = N_TP * 4 * PAD
    pick = lax.broadcasted_iota(jnp.int32, (width, lanes), 0) == source_ref[...]
    pick = jnp.where(pick, 1.0, 0.0).astype(jnp.bfloat16)
    for m in range(D // width):
        for which, ref in enumerate((gate_ref, up_ref, down_ref)):
            moved = dot(ref[:, m * width : (m + 1) * width], pick).astype(jnp.bfloat16)
            for t in range(N_TP):
                piece = moved[:, t * 128 : (t + 1) * 128]
                if which < 2:
                    mix_ref[t, which, :, m * 128 : (m + 1) * 128] = piece
                else:
                    out_ref[t, :, m * 128 : (m + 1) * 128] = piece


def regroup(source, gate_t, up_t, down):
    vmem = pl.BlockSpec(memory_space=pltpu.VMEM)
    return pl.pallas_call(
        regroup_kernel,
        out_shape=(
            jax.ShapeDtypeStruct((N_TP, 2, FF, 1024), jnp.bfloat16),
            jax.ShapeDtypeStruct((N_TP, FF, 1024), jnp.bfloat16),
        ),
        in_specs=[vmem] * 4,
        out_specs=(vmem, vmem),
        compiler_params=pltpu.CompilerParams(vmem_limit_bytes=40 * 2**20),
        cost_estimate=pl.CostEstimate(
            flops=2 * 3 * FF * D * 1024, bytes_accessed=7 * 2**20, transcendentals=0
        ),
        name="regroup",
    )(source, gate_t, up_t, down)


def swap(x, axes):
    return lax.all_to_all(x, axes, 0, 0, tiled=True)


def spread(x, axes, count):
    return swap(jnp.broadcast_to(x[None], (count, *x.shape)), axes)


def other_core(x):
    return lax.ppermute(x, "c", [(0, 1), (1, 0)])


def pad_pieces(x):
    lead = x.shape[0] // PIECE
    x = x.reshape(lead, PIECE, *x.shape[1:])
    x = jnp.pad(x, ((0, 0), (0, PAD - PIECE)) + ((0, 0),) * (x.ndim - 2))
    return x.reshape(lead * PAD, *x.shape[2:])


def split_sum(x):
    high = x.astype(jnp.bfloat16)
    return high, (x - high.astype(jnp.float32)).astype(jnp.bfloat16)


def body(
    queries, new_latent, cache, cache_lengths, w_uv, w_o, residual, norm_gain, w_gate, w_up, w_down
):
    core = lax.axis_index("c")
    dp_index = lax.axis_index(DP)
    tp_index = lax.axis_index(TP)

    lane = np.arange(N_TP * 4 * PAD)
    lane_t, lane_core, lane_u, lane_j = lane // 128, lane // 64 % 2, lane // 32 % 2, lane % PAD
    base = jnp.asarray(lane_u * 2 * FEAT + lane_t * PIECE + lane_j, jnp.int32)
    source = base + (jnp.asarray(lane_core, jnp.int32) ^ core) * FEAT
    source = jnp.where(jnp.asarray(lane_j < PIECE), source, -1)[None, :]
    mix_w, down_w = regroup(source, w_gate.T, w_up.T, w_down)
    mix_w = swap(mix_w, TP).reshape(N_TP * 2 * FF, 1024)
    down_w = swap(down_w, TP).reshape(N_TP * FF, 1024)

    own_lengths = lax.dynamic_index_in_dim(cache_lengths, dp_index, 0, keepdims=False)
    ends = jnp.cumsum(own_lengths)
    bounds = jnp.concatenate([ends - own_lengths, ends]).astype(jnp.int32)
    fresh = jnp.transpose(new_latent, (1, 0, 2)).reshape(NEW, KDIM)
    heads = attend(bounds, queries.reshape(ROWS, KDIM), fresh, cache.T, w_uv)

    heads = swap(heads, "c").reshape(2 * NEW, HEADS // 2 * VDIM)
    heads = spread(heads, RING, N_RING).reshape(TOKENS, HEADS // 2 * VDIM)
    more_heads = other_core(heads)
    w_ot = pad_pieces(w_o.T)
    half = HEADS // 2 * VDIM
    w_own = lax.dynamic_slice_in_dim(w_ot, core * half, half, 1)
    w_more = lax.dynamic_slice_in_dim(w_ot, (1 - core) * half, half, 1)
    partial = dot(w_own, heads, NT) + dot(w_more, more_heads, NT)
    partial = partial.astype(jnp.bfloat16).reshape(N_TP, PAD, TOKENS)
    attended = jnp.sum(swap(partial, TP).astype(jnp.float32), axis=0)
    updated = (pad_pieces(residual.T).astype(jnp.float32) + attended).astype(jnp.bfloat16)

    wide = updated.astype(jnp.float32)
    gain = lax.dynamic_slice_in_dim(norm_gain, dp_index * FEAT + tp_index * PIECE, PIECE, 0)
    scaled = (wide[:PIECE] * gain.astype(jnp.float32)[:, None]).astype(jnp.bfloat16)
    high, low = split_sum(jnp.sum(wide * wide, axis=0, keepdims=True))
    block = jnp.concatenate([scaled, high, low, jnp.zeros((2, TOKENS), jnp.bfloat16)], axis=0)
    own = spread(block, RING, N_RING)
    more = other_core(own)

    def squares(x):
        return jnp.sum(x[:, PIECE : PIECE + 2].astype(jnp.float32), axis=(0, 1))

    high, low = split_sum((squares(own) + squares(more))[None])
    features = jnp.stack([own.reshape(8, 64, TOKENS), more.reshape(8, 64, TOKENS)], axis=1)
    mix = dot(mix_w, features.reshape(1024, TOKENS)).astype(jnp.bfloat16)
    tail = jnp.concatenate([high, low, jnp.zeros((6, TOKENS), jnp.bfloat16)], axis=0)
    mix = jnp.concatenate(
        [mix.reshape(N_TP, 2 * FF, TOKENS), jnp.broadcast_to(tail, (N_TP, 8, TOKENS))], axis=1
    )
    mix = jnp.sum(swap(mix, TP).astype(jnp.float32), axis=0)
    mean = (mix[2 * FF] + mix[2 * FF + 1]) * (1.0 / D)
    inverse_rms = lax.rsqrt(mean + EPS)[None]
    gate_out = mix[:FF] * inverse_rms
    up_out = mix[FF : 2 * FF] * inverse_rms
    hidden = (jax.nn.silu(gate_out) * up_out).astype(jnp.bfloat16)
    hidden = spread(hidden, TP, N_TP).reshape(N_TP * FF, TOKENS)

    term = dot(down_w, hidden, TN).reshape(8, 2, 64, TOKENS)
    term = term[:, 0] + other_core(term[:, 1].astype(jnp.bfloat16)).astype(jnp.float32)
    term = swap(term.astype(jnp.bfloat16).reshape(N_RING, PAD, TOKENS), RING)
    term = jnp.sum(term.astype(jnp.float32), axis=0)
    return (wide[:PIECE] + term[:PIECE]).astype(jnp.bfloat16).T


def solution(mesh):
    parts = Mesh(mesh.devices.reshape(tuple(SIZES.values())), tuple(SIZES))
    everywhere = DP + TP
    return jax.shard_map(
        body,
        mesh=parts,
        in_specs=(
            P(DP, None, TP, None),
            P(DP, None, None),
            P(DP, None),
            P(),
            P(TP, None, None),
            P(TP, DP),
            P(None, everywhere),
            P(),
            P(None, everywhere),
            P(None, everywhere),
            P(everywhere, None),
        ),
        out_specs=P(None, everywhere),
        check_vma=False,
    )
```

```python
import functools

import jax
import jax.numpy as jnp
from jax import lax
from jax.experimental import pallas as pl
from jax.experimental.pallas import tpu as pltpu
from jax.sharding import Mesh, PartitionSpec as P

DP = ("xl", "z", "c")
RING = ("xl", "z")
TP = ("xh", "y")
SIZES = {"xl": 2, "z": 8, "c": 2, "xh": 2, "y": 4}
N_RING, N_TP, N_Y = 16, 8, 4

STEPS, HEADS, REQ = 3, 16, 4
NEW = REQ * STEPS
ROWS = NEW * HEADS
TOKENS = 384
LAT, KDIM, VDIM = 512, 576, 128
HALF = HEADS // 2 * VDIM
CTX, CHUNK = 4096, 512
N_CHUNK = CTX // CHUNK
D, FEAT, PIECE, PAD = 7168, 224, 28, 32
PAIR = 2 * PIECE
SIDE = N_RING * PAIR
OUT = N_RING * 2 * PAD
FF, ROOM = 72, 80
EPS = 1e-06
LOG2E = 1.4426950408889634
SCALE = 192.0 ** (-0.5)
NEG = -1e30

NT = (((1,), (1,)), ((), ()))
TN = (((0,), (0,)), ((), ()))

VMEM = pl.BlockSpec(memory_space=pltpu.VMEM)
SMEM = pl.BlockSpec(memory_space=pltpu.SMEM)
ANY = pl.BlockSpec(memory_space=pl.ANY)


def params(mib=40):
    return pltpu.CompilerParams(vmem_limit_bytes=mib * 2**20)


def shape(*dims, dtype=jnp.bfloat16):
    return jax.ShapeDtypeStruct(dims, dtype)


def dot(a, b, dims=(((1,), (0,)), ((), ()))):
    return lax.dot_general(a, b, dims, preferred_element_type=jnp.float32)


def attend_kernel(
    lengths, q_ref, fresh_ref, cache_hbm, w_uv_hbm, mine_ref, theirs_ref, keys, scores, w_uv,
    new_keys, key_sems, w_sem,
):
    copies = [
        pltpu.make_async_copy(
            cache_hbm.at[:, pl.ds(j * CHUNK, CHUNK)], keys.at[j], key_sems.at[j]
        )
        for j in range(N_CHUNK)
    ]
    w_copy = pltpu.make_async_copy(w_uv_hbm, w_uv, w_sem)
    for copy in copies:
        copy.start()
    w_copy.start()

    dp_index = lax.axis_index(DP)
    q = q_ref[...]
    row = lax.broadcasted_iota(jnp.int32, (ROWS, 1), 0)
    request = row // (STEPS * HEADS)
    step = row // HEADS - request * STEPS
    low = jnp.zeros((ROWS, 1), jnp.int32)
    high = jnp.zeros((ROWS, 1), jnp.int32)
    start = 0
    for r in range(REQ):
        end = start + lengths[r, dp_index]
        low = jnp.where(request == r, start, low)
        high = jnp.where(request == r, end, high)
        start = end

    new_keys[...] = jnp.zeros_like(new_keys)
    for i in range(STEPS):
        new_keys[i * REQ : (i + 1) * REQ, :] = fresh_ref[i].astype(jnp.float32)
    fresh = new_keys[...].astype(jnp.bfloat16)
    key = lax.broadcasted_iota(jnp.int32, (ROWS, 16), 1)
    key_step = key // REQ
    seen = (key - key_step * REQ == request) & (key_step <= step)
    fresh_scores = jnp.where(seen, dot(q, fresh, NT) * (SCALE * LOG2E), NEG)
    top = jnp.max(fresh_scores, axis=1, keepdims=True)

    for j in range(N_CHUNK):
        copies[j].wait()
        slot = j * CHUNK + lax.broadcasted_iota(jnp.int32, (ROWS, CHUNK), 1)
        part = dot(q, keys[j]) * (SCALE * LOG2E)
        part = jnp.where((slot >= low) & (slot < high), part, NEG)
        scores[j] = part
        top = jnp.maximum(top, jnp.max(part, axis=1, keepdims=True))

    weights = jnp.exp2(fresh_scores - top)
    total = jnp.sum(weights, axis=1, keepdims=True)
    mixed = dot(weights.astype(jnp.bfloat16), fresh[:, :LAT])
    for j in range(N_CHUNK):
        weights = jnp.exp2(scores[j] - top)
        total = total + jnp.sum(weights, axis=1, keepdims=True)
        mixed = mixed + dot(weights.astype(jnp.bfloat16), keys[j, :LAT, :], NT)
    mixed = (mixed / total).astype(jnp.bfloat16)

    w_copy.wait()
    head = row - (row // HEADS) * HEADS
    halves = []
    for half in range(2):
        values = []
        for h in range(half * HEADS // 2, (half + 1) * HEADS // 2):
            value = jnp.where(head == h, dot(mixed, w_uv[h]), 0.0)
            values.append(jnp.sum(value.reshape(NEW, HEADS, VDIM), axis=1))
        halves.append(jnp.concatenate(values, axis=1))
    second = lax.axis_index("c") == 1
    mine_ref[...] = jnp.where(second, halves[1], halves[0]).astype(jnp.bfloat16)
    theirs_ref[...] = jnp.where(second, halves[0], halves[1]).astype(jnp.bfloat16)


def attend(lengths, q, fresh, cache_t, w_uv):
    return pl.pallas_call(
        attend_kernel,
        out_shape=(shape(NEW, HALF), shape(NEW, HALF)),
        in_specs=[SMEM, VMEM, VMEM, ANY, ANY],
        out_specs=(VMEM, VMEM),
        scratch_shapes=[
            pltpu.VMEM((N_CHUNK, KDIM, CHUNK), jnp.bfloat16),
            pltpu.VMEM((N_CHUNK, ROWS, CHUNK), jnp.float32),
            pltpu.VMEM((HEADS, LAT, VDIM), jnp.bfloat16),
            pltpu.VMEM((16, KDIM), jnp.float32),
            pltpu.SemaphoreType.DMA((N_CHUNK,)),
            pltpu.SemaphoreType.DMA,
        ],
        compiler_params=params(58),
        cost_estimate=pl.CostEstimate(
            flops=2 * ROWS * CTX * (KDIM + LAT), bytes_accessed=7 * 2**20, transcendentals=ROWS * CTX
        ),
        name="attend",
    )(lengths, q, fresh, cache_t, w_uv)


def fan_kernel(mine_ref, theirs_ref, out_ref):
    second = lax.axis_index("c") == 1
    mine, theirs = mine_ref[...].astype(jnp.float32), theirs_ref[...].astype(jnp.float32)
    both = jnp.concatenate(
        [jnp.where(second, theirs, mine), jnp.where(second, mine, theirs)], axis=0
    ).astype(jnp.bfloat16)
    for i in range(N_RING):
        out_ref[i] = both


def fan(mine, theirs):
    return pl.pallas_call(
        fan_kernel,
        out_shape=shape(N_RING, 2 * NEW, HALF),
        in_specs=[VMEM, VMEM],
        out_specs=VMEM,
        compiler_params=params(),
        name="fan",
    )(mine, theirs)


def pick_columns(piece, width):
    lane = lax.broadcasted_iota(jnp.int32, (1, N_Y * 8 * piece), 1)
    k, rest = lane // (8 * piece), lane % (8 * piece)
    side, rest = rest // (4 * piece), rest % (4 * piece)
    u, rest = rest // (2 * piece), rest % (2 * piece)
    xh, j = rest // piece, rest % piece
    source = (2 * u + (side ^ lax.axis_index("c"))) * FEAT
    source = source + (xh * N_Y + (k ^ lax.axis_index("y"))) * PIECE + j
    source = jnp.where(j < PIECE, source, -1)
    rows = lax.broadcasted_iota(jnp.int32, (width, N_Y * 8 * piece), 0)
    return jnp.where(rows == source, 1.0, 0.0).astype(jnp.bfloat16)


def regroup_kernel(gate_ref, up_ref, down_ref, gain_ref, _, *refs):
    mix_refs, down_refs, rows = refs[:N_Y], refs[N_Y:-1], refs[-1]
    gain = gain_ref[...].astype(jnp.float32)
    for i, ref in enumerate((gate_ref, up_ref)):
        rows[i * ROOM + ROOM - 16 : (i + 1) * ROOM, :] = jnp.zeros((16, D), jnp.bfloat16)
        rows[i * ROOM : i * ROOM + FF, :] = (ref[...].astype(jnp.float32) * gain).astype(jnp.bfloat16)
    rows[3 * ROOM - 16 : 3 * ROOM, :] = jnp.zeros((16, D), jnp.bfloat16)
    rows[2 * ROOM : 2 * ROOM + FF, :] = down_ref[...]
    width = 4 * FEAT
    for first, last, refs, piece in ((0, 2 * ROOM, mix_refs, PIECE), (2 * ROOM, 3 * ROOM, down_refs, PAD)):
        pick = pick_columns(piece, width)
        size = 4 * piece
        for m in range(D // width):
            moved = dot(rows[first:last, m * width : (m + 1) * width], pick).astype(jnp.bfloat16)
            for k in range(N_Y):
                for side in range(2):
                    at, to = (2 * k + side) * size, (side * 8 + m) * size
                    refs[k][:, to : to + size] = moved[:, at : at + size]


def regroup(gate_t, up_t, down, gain, after):
    return pl.pallas_call(
        regroup_kernel,
        out_shape=[shape(2 * ROOM, 2 * SIDE)] * N_Y + [shape(ROOM, 2 * OUT)] * N_Y,
        in_specs=[VMEM] * 4 + [ANY],
        out_specs=[VMEM] * (2 * N_Y),
        scratch_shapes=[pltpu.VMEM((3 * ROOM, D), jnp.bfloat16)],
        compiler_params=params(),
        cost_estimate=pl.CostEstimate(
            flops=2 * 3 * ROOM * D * 1024, bytes_accessed=7 * 2**20, transcendentals=0
        ),
        name="regroup",
    )(gate_t, up_t, down, gain, after)


def project_kernel(first_ref, heads_ref, w_ref, out_ref):
    lanes = pl.ds(pl.multiple_of((1 - lax.axis_index("c")) * HALF, HALF), HALF)
    total = first_ref[...] + dot(w_ref[:, lanes], heads_ref[...], NT)
    total = total.astype(jnp.bfloat16)
    out_ref[0] = total
    out_ref[1] = total


def project(first, heads, w_ot):
    return pl.pallas_call(
        project_kernel,
        out_shape=shape(2, FEAT, TOKENS),
        in_specs=[VMEM, VMEM, VMEM],
        out_specs=VMEM,
        compiler_params=params(),
        name="project",
    )(first, heads, w_ot)


def update_kernel(parts_ref, residual_ref, updated_ref, out_ref):
    attended = jnp.sum(parts_ref[...].astype(jnp.float32), axis=0)
    updated = (residual_ref[...].astype(jnp.float32) + attended).astype(jnp.bfloat16)
    updated_ref[...] = updated
    for i in range(N_RING):
        out_ref[i] = updated


def update(parts, residual):
    return pl.pallas_call(
        update_kernel,
        out_shape=(shape(PAIR, TOKENS), shape(N_RING, PAIR, TOKENS)),
        in_specs=[VMEM] * 2,
        out_specs=(VMEM, VMEM),
        compiler_params=params(),
        name="update",
    )(parts, residual)


def squares_of(ref):
    wide = ref[...].astype(jnp.float32)
    return jnp.sum(wide * wide, axis=(0, 1))[None]


def mix_own_kernel(own_ref, *refs):
    blocks, (out_ref, squares_ref, held, sems) = refs[:N_Y], refs[N_Y:]
    copies = [
        pltpu.make_async_copy(blocks[k].at[:, pl.ds(0, SIDE)], held.at[k], sems.at[k])
        for k in range(N_Y)
    ]
    for copy in copies:
        copy.start()
    squares_ref[...] = squares_of(own_ref)
    own = own_ref[...].reshape(SIDE, TOKENS)
    for k in range(N_Y):
        copies[k].wait()
        out_ref[k] = dot(held[k], own)


def mix_more_kernel(part_ref, squares_ref, more_ref, *refs):
    blocks, (out_ref, held, sems) = refs[:N_Y], refs[N_Y:]
    copies = [
        pltpu.make_async_copy(blocks[k].at[:, pl.ds(SIDE, SIDE)], held.at[k], sems.at[k])
        for k in range(N_Y)
    ]
    for copy in copies:
        copy.start()
    squares = squares_ref[...] + squares_of(more_ref)
    more = more_ref[...].reshape(SIDE, TOKENS)
    high = squares.astype(jnp.bfloat16).astype(jnp.float32)
    row = lax.broadcasted_iota(jnp.int32, (2 * ROOM, TOKENS), 0)
    y = lax.axis_index("y")
    for k in range(N_Y):
        copies[k].wait()
        part = part_ref[k] + dot(held[k], more)
        part = jnp.where(row == FF, high, jnp.where(row == FF + 1, squares - high, part))
        out_ref[y ^ k] = part.astype(jnp.bfloat16)


def mix(own, more, blocks):
    scratch = [
        pltpu.VMEM((N_Y, 2 * ROOM, SIDE), jnp.bfloat16),
        pltpu.SemaphoreType.DMA((N_Y,)),
    ]
    cost = pl.CostEstimate(
        flops=2 * N_Y * 2 * ROOM * SIDE * TOKENS, bytes_accessed=4 * 2**20, transcendentals=0
    )
    part, squares = pl.pallas_call(
        mix_own_kernel,
        out_shape=(
            shape(N_Y, 2 * ROOM, TOKENS, dtype=jnp.float32),
            shape(1, TOKENS, dtype=jnp.float32),
        ),
        in_specs=[VMEM] + [ANY] * N_Y,
        out_specs=(VMEM, VMEM),
        scratch_shapes=scratch,
        compiler_params=params(),
        cost_estimate=cost,
        name="mix_own",
    )(own, *blocks)
    return pl.pallas_call(
        mix_more_kernel,
        out_shape=shape(N_Y, 2 * ROOM, TOKENS),
        in_specs=[VMEM] * 3 + [ANY] * N_Y,
        out_specs=VMEM,
        scratch_shapes=scratch,
        compiler_params=params(),
        cost_estimate=cost,
        name="mix_more",
    )(part, squares, more, *blocks)


def gate_kernel(parts_ref, out_ref):
    total = jnp.sum(parts_ref[...].astype(jnp.float32), axis=0)
    mean = (total[FF : FF + 1] + total[FF + 1 : FF + 2]) * (1.0 / D)
    inverse_rms = lax.rsqrt(mean + EPS)
    gate_out, up_out = total[:ROOM] * inverse_rms, total[ROOM:] * inverse_rms
    row = lax.broadcasted_iota(jnp.int32, (ROOM, TOKENS), 0)
    hidden = jnp.where(row < FF, gate_out / (1.0 + jnp.exp(-gate_out)) * up_out, 0.0)
    hidden = hidden.astype(jnp.bfloat16)
    for t in range(N_Y):
        out_ref[t] = hidden


def gate(parts):
    return pl.pallas_call(
        gate_kernel,
        out_shape=shape(N_Y, ROOM, TOKENS),
        in_specs=[VMEM],
        out_specs=VMEM,
        compiler_params=params(),
        name="gate",
    )(parts)


def down_kernel(side, hidden_ref, *refs):
    blocks, (out_ref, held, hidden, sems) = refs[:N_Y], refs[N_Y:]
    copies = [
        pltpu.make_async_copy(
            blocks[k].at[:, pl.ds(side * OUT, OUT)], held.at[pl.ds(k * ROOM, ROOM), :], sems.at[k]
        )
        for k in range(N_Y)
    ]
    for copy in copies:
        copy.start()
    y = lax.axis_index("y")
    for k in range(N_Y):
        hidden[k * ROOM : (k + 1) * ROOM, :] = hidden_ref[y ^ k]
    for copy in copies:
        copy.wait()
    out_ref[...] = dot(held[...], hidden[...], TN).astype(out_ref.dtype)


def down(side, hidden, blocks):
    return pl.pallas_call(
        functools.partial(down_kernel, side),
        out_shape=shape(OUT, TOKENS, dtype=jnp.bfloat16 if side else jnp.float32),
        in_specs=[VMEM] + [ANY] * N_Y,
        out_specs=VMEM,
        scratch_shapes=[
            pltpu.VMEM((N_Y * ROOM, OUT), jnp.bfloat16),
            pltpu.VMEM((N_Y * ROOM, TOKENS), jnp.bfloat16),
            pltpu.SemaphoreType.DMA((N_Y,)),
        ],
        compiler_params=params(),
        cost_estimate=pl.CostEstimate(
            flops=2 * N_Y * ROOM * OUT * TOKENS, bytes_accessed=3 * 2**20, transcendentals=0
        ),
        name="down",
    )(hidden, *blocks)


def swap(x, axes):
    return lax.all_to_all(x, axes, 0, 0, tiled=True)


def other_core(x):
    return lax.ppermute(x, "c", [(0, 1), (1, 0)])


def other_half(x):
    return lax.ppermute(x, "xh", [(0, 1), (1, 0)])


def body(
    queries, new_latent, cache, cache_lengths, w_uv, w_o, residual, norm_gain, w_gate, w_up, w_down
):
    core, xh = lax.axis_index("c"), lax.axis_index("xh")

    fresh = jnp.transpose(new_latent, (1, 0, 2))
    mine, theirs = attend(
        cache_lengths.T, queries.reshape(ROWS, KDIM), fresh, cache.T, w_uv
    )

    blocks = regroup(w_gate.T, w_up.T, w_down, norm_gain[None], mine)
    mix_blocks, down_blocks = list(blocks[:N_Y]), list(blocks[N_Y:])

    def exchange(blocks, which):
        for k in which:
            blocks[k] = lax.ppermute(blocks[k], "y", [(i, i ^ k) for i in range(N_Y)])

    def fence(*x):
        out = lax.optimization_barrier((*x, *mix_blocks, *down_blocks))
        mix_blocks[:], down_blocks[:] = out[-2 * N_Y : -N_Y], out[-N_Y:]
        return out[: -2 * N_Y]

    partner = other_half(residual.T)
    residual = jnp.concatenate(
        [jnp.where(xh == 0, residual.T, partner), jnp.where(xh == 0, partner, residual.T)], axis=0
    )
    w_ot = w_o.T.reshape(2, N_Y, PIECE, HEADS * VDIM).transpose(1, 0, 2, 3)
    w_ot = w_ot.reshape(FEAT, HEADS * VDIM)
    w_own = lax.dynamic_slice_in_dim(w_ot, core * HALF, HALF, 1)

    heads = swap(fan(mine, other_core(theirs)), RING).reshape(TOKENS, HALF)
    exchange(mix_blocks, (1, 3))
    heads, residual, w_ot, w_own = fence(heads, residual, w_ot, w_own)
    more_heads = other_core(heads)
    first = dot(w_own, heads, NT)
    exchange(down_blocks, (2,))
    (partial,) = fence(project(first, more_heads, w_ot))

    updated, block = update(swap(partial.reshape(N_TP, PAIR, TOKENS), TP), residual)
    exchange(mix_blocks, (2,))
    exchange(down_blocks, (1, 3))
    (own,) = fence(swap(block, RING))
    hidden = gate(swap(mix(own, other_core(own), mix_blocks), "y"))
    hidden = swap(hidden, "y")
    more = other_core(down(1, hidden, down_blocks))
    term = down(0, hidden, down_blocks) + more.astype(jnp.float32)
    term = swap(term.astype(jnp.bfloat16).reshape(2 * N_RING, PAD, TOKENS), RING + ("xh",))
    term = jnp.sum(term.astype(jnp.float32), axis=0)[:PIECE]
    updated = jnp.where(xh == 0, updated[:PIECE], updated[PIECE:])
    return (updated.astype(jnp.float32) + term).astype(jnp.bfloat16).T


def solution(mesh):
    parts = Mesh(mesh.devices.reshape(tuple(SIZES.values())), tuple(SIZES))
    everywhere = DP + TP
    return jax.shard_map(
        body,
        mesh=parts,
        in_specs=(
            P(DP, None, TP, None),
            P(DP, None, None),
            P(DP, None),
            P(),
            P(TP, None, None),
            P(TP, DP),
            P(None, everywhere),
            P(),
            P(None, everywhere),
            P(None, everywhere),
            P(everywhere, None),
        ),
        out_specs=P(None, everywhere),
        check_vma=False,
    )
```

```python
import functools

import jax
import jax.numpy as jnp
from jax import lax
from jax.experimental import pallas as pl
from jax.experimental.pallas import tpu as pltpu
from jax.sharding import Mesh, PartitionSpec as P

DP = ("xl", "z", "c")
RING = ("xl", "z")
TP = ("xh", "y")
SIZES = {"xl": 2, "z": 8, "c": 2, "xh": 2, "y": 4}
N_RING, N_TP, N_Y = 16, 8, 4

STEPS, HEADS, REQ = 3, 16, 4
NEW = REQ * STEPS
ROWS = NEW * HEADS
TOKENS = 384
LAT, KDIM, VDIM = 512, 576, 128
HALF = HEADS // 2 * VDIM
CTX, CHUNK = 4096, 1024
N_CHUNK = CTX // CHUNK
D, FEAT, PIECE, PAD = 7168, 224, 28, 32
PAIR = 2 * PIECE
SIDE = N_RING * PAIR
OUT = N_RING * 2 * PAD
FF, ROOM = 72, 80
EPS = 1e-06
LOG2E = 1.4426950408889634
SCALE = 192.0 ** (-0.5)
NEG = -1e30

NT = (((1,), (1,)), ((), ()))
TN = (((0,), (0,)), ((), ()))

VMEM = pl.BlockSpec(memory_space=pltpu.VMEM)
SMEM = pl.BlockSpec(memory_space=pltpu.SMEM)
ANY = pl.BlockSpec(memory_space=pl.ANY)
HBM = pl.BlockSpec(memory_space=pltpu.HBM)


def params(mib=24):
    return pltpu.CompilerParams(vmem_limit_bytes=mib * 2**20)


def shape(*dims, dtype=jnp.bfloat16):
    return jax.ShapeDtypeStruct(dims, dtype)


def dot(a, b, dims=(((1,), (0,)), ((), ()))):
    return lax.dot_general(a, b, dims, preferred_element_type=jnp.float32)


def attend_kernel(
    lengths, q_ref, fresh_ref, cache_hbm, w_uv_hbm, mine_ref, theirs_ref, keys, scores, w_uv,
    new_keys, key_sems, w_sem,
):
    copies = [
        pltpu.make_async_copy(
            cache_hbm.at[:, pl.ds(j * CHUNK, CHUNK)], keys.at[j], key_sems.at[j]
        )
        for j in range(N_CHUNK)
    ]
    w_copy = pltpu.make_async_copy(w_uv_hbm, w_uv, w_sem)
    for copy in copies:
        copy.start()

    dp_index = lax.axis_index(DP)
    q = q_ref[...]
    row = lax.broadcasted_iota(jnp.int32, (ROWS, 1), 0)
    request = row // (STEPS * HEADS)
    step = row // HEADS - request * STEPS
    low = jnp.zeros((ROWS, 1), jnp.int32)
    high = jnp.zeros((ROWS, 1), jnp.int32)
    start = 0
    for r in range(REQ):
        end = start + lengths[r, dp_index]
        low = jnp.where(request == r, start, low)
        high = jnp.where(request == r, end, high)
        start = end

    new_keys[...] = jnp.zeros_like(new_keys)
    for i in range(STEPS):
        new_keys[i * REQ : (i + 1) * REQ, :] = fresh_ref[i].astype(jnp.float32)
    fresh = new_keys[...].astype(jnp.bfloat16)
    key = lax.broadcasted_iota(jnp.int32, (ROWS, 16), 1)
    key_step = key // REQ
    seen = (key - key_step * REQ == request) & (key_step <= step)
    fresh_scores = jnp.where(seen, dot(q, fresh, NT) * (SCALE * LOG2E), NEG)
    top = jnp.max(fresh_scores, axis=1, keepdims=True)

    tops = jnp.full((ROWS, 128), NEG, jnp.float32)
    for j in range(N_CHUNK):
        copies[j].wait()
        if j == 1:
            w_copy.start()
        slot = j * CHUNK + lax.broadcasted_iota(jnp.int32, (ROWS, CHUNK), 1)
        part = dot(q, keys[j]) * (SCALE * LOG2E)
        part = jnp.where((slot >= low) & (slot < high), part, NEG)
        scores[j] = part
        for i in range(0, CHUNK, 128):
            tops = jnp.maximum(tops, part[:, i : i + 128])
    top = jnp.maximum(top, jnp.max(tops, axis=1, keepdims=True))

    totals = jnp.zeros((ROWS, 128), jnp.float32)
    weights = jnp.exp2(fresh_scores - top)
    total = jnp.sum(weights, axis=1, keepdims=True)
    mixed = dot(weights.astype(jnp.bfloat16), fresh[:, :LAT])
    for j in range(N_CHUNK):
        weights = jnp.exp2(scores[j] - top)
        for i in range(0, CHUNK, 128):
            totals = totals + weights[:, i : i + 128]
        mixed = mixed + dot(weights.astype(jnp.bfloat16), keys[j, :LAT, :], NT)
    total = total + jnp.sum(totals, axis=1, keepdims=True)
    mixed = (mixed / total).astype(jnp.bfloat16)

    w_copy.wait()
    head = row - (row // HEADS) * HEADS
    halves = []
    for half in range(2):
        values = []
        for h in range(half * HEADS // 2, (half + 1) * HEADS // 2, 2):
            pair = dot(mixed, jnp.concatenate([w_uv[h], w_uv[h + 1]], axis=1))
            for i in range(2):
                value = jnp.where(head == h + i, pair[:, i * VDIM : (i + 1) * VDIM], 0.0)
                values.append(jnp.sum(value.reshape(NEW, HEADS, VDIM), axis=1))
        halves.append(jnp.concatenate(values, axis=1))
    second = lax.axis_index("c") == 1
    mine_ref[...] = jnp.where(second, halves[1], halves[0]).astype(jnp.bfloat16)
    theirs_ref[...] = jnp.where(second, halves[0], halves[1]).astype(jnp.bfloat16)


def attend(lengths, q, fresh, cache_t, w_uv):
    return pl.pallas_call(
        attend_kernel,
        out_shape=(shape(NEW, HALF), shape(NEW, HALF)),
        in_specs=[SMEM, VMEM, VMEM, ANY, ANY],
        out_specs=(VMEM, VMEM),
        scratch_shapes=[
            pltpu.VMEM((N_CHUNK, KDIM, CHUNK), jnp.bfloat16),
            pltpu.VMEM((N_CHUNK, ROWS, CHUNK), jnp.float32),
            pltpu.VMEM((HEADS, LAT, VDIM), jnp.bfloat16),
            pltpu.VMEM((16, KDIM), jnp.float32),
            pltpu.SemaphoreType.DMA((N_CHUNK,)),
            pltpu.SemaphoreType.DMA,
        ],
        compiler_params=params(58),
        cost_estimate=pl.CostEstimate(
            flops=2 * ROWS * CTX * (KDIM + LAT), bytes_accessed=7 * 2**20, transcendentals=ROWS * CTX
        ),
        name="attend",
    )(lengths, q, fresh, cache_t, w_uv)


def fan_kernel(mine_ref, theirs_ref, out_ref):
    second = lax.axis_index("c") == 1
    mine, theirs = mine_ref[...].astype(jnp.float32), theirs_ref[...].astype(jnp.float32)
    both = jnp.concatenate(
        [jnp.where(second, theirs, mine), jnp.where(second, mine, theirs)], axis=0
    ).astype(jnp.bfloat16)
    for i in range(N_RING):
        out_ref[i] = both


def fan(mine, theirs):
    return pl.pallas_call(
        fan_kernel,
        out_shape=shape(N_RING, 2 * NEW, HALF),
        in_specs=[VMEM, VMEM],
        out_specs=VMEM,
        compiler_params=params(),
        name="fan",
    )(mine, theirs)


def pick_columns(ks, width):
    lanes = len(ks) * 8 * PAD
    lane = lax.broadcasted_iota(jnp.int32, (1, lanes), 1)
    n, side, u = lane // (8 * PAD), lane // (4 * PAD) % 2, lane // (2 * PAD) % 2
    k = jnp.zeros_like(n)
    for i in range(len(ks)):
        k = jnp.where(n == i, ks[i], k)
    xh, j = lane // PAD % 2, lane % PAD
    source = (2 * u + (side ^ lax.axis_index("c"))) * FEAT
    source = source + (xh * N_Y + (k ^ lax.axis_index("y"))) * PIECE + j
    source = jnp.where(j < PIECE, source, -1)
    rows = lax.broadcasted_iota(jnp.int32, (width, lanes), 0)
    return jnp.where(rows == source, 1.0, 0.0).astype(jnp.bfloat16)


def regroup_kernel(ks, count, gained, *refs):
    sources, gain_ref, refs = refs[:count], refs[count], refs[count + 2 :]
    outs, (rows, loaded, moved_ref, in_sems, out_sems) = refs[:-5], refs[-5:]
    width = 4 * FEAT
    loads = [
        pltpu.make_async_copy(source, loaded.at[i], in_sems.at[i])
        for i, source in enumerate(sources)
    ]
    for load in loads:
        load.start()
    pick = pick_columns(ks, width)
    for i in range(count):
        loads[i].wait()
        rows[i * ROOM + ROOM - 16 : (i + 1) * ROOM, :] = jnp.zeros((16, D), jnp.bfloat16)
        if gained:
            for j in range(D // 128):
                lanes = slice(j * 128, (j + 1) * 128)
                wide = loaded[i, :, lanes].astype(jnp.float32)
                wide = wide * gain_ref[j : j + 1, :].astype(jnp.float32)
                rows[i * ROOM : i * ROOM + FF, lanes] = wide.astype(jnp.bfloat16)
        else:
            rows[i * ROOM : i * ROOM + FF, :] = loaded[i]
    stores = []
    for n in range(len(ks)):
        for m in range(D // width):
            moved = dot(rows[:, m * width : (m + 1) * width], pick[:, n * 256 : (n + 1) * 256])
            moved = moved.astype(jnp.bfloat16)
            for side in range(2):
                to = (side * 8 + m) * 128
                moved_ref[n, :, to : to + 128] = moved[:, side * 128 : (side + 1) * 128]
        stores.append(pltpu.make_async_copy(moved_ref.at[n], outs[n], out_sems.at[n]))
        stores[-1].start()
    for store in stores:
        store.wait()


def regroup(ks, sources, gain, gained, after):
    count = len(sources)
    return pl.pallas_call(
        functools.partial(regroup_kernel, ks, count, gained),
        out_shape=[shape(count * ROOM, 2 * OUT)] * len(ks),
        in_specs=[HBM] * count + [VMEM, ANY],
        out_specs=[HBM] * len(ks),
        scratch_shapes=[
            pltpu.VMEM((count * ROOM, D), jnp.bfloat16),
            pltpu.VMEM((count, FF, D), jnp.bfloat16),
            pltpu.VMEM((len(ks), count * ROOM, 2 * OUT), jnp.bfloat16),
            pltpu.SemaphoreType.DMA((count,)),
            pltpu.SemaphoreType.DMA((len(ks),)),
        ],
        compiler_params=params(58),
        cost_estimate=pl.CostEstimate(
            flops=2 * count * ROOM * D * 256 * len(ks), bytes_accessed=5 * 2**20, transcendentals=0
        ),
        name="regroup",
    )(*sources, gain, after)


def project_own_kernel(heads_ref, w_ref, out_ref):
    lanes = pl.ds(pl.multiple_of(lax.axis_index("c") * HALF, HALF), HALF)
    out_ref[...] = dot(w_ref[:, lanes], heads_ref[...], NT)


def project_more_kernel(first_ref, heads_ref, w_ref, out_ref):
    lanes = pl.ds(pl.multiple_of((1 - lax.axis_index("c")) * HALF, HALF), HALF)
    total = first_ref[...] + dot(w_ref[:, lanes], heads_ref[...], NT)
    pieces = [total[t * PIECE : (t + 1) * PIECE] for t in range(N_TP)]
    for y in range(N_Y):
        pair = jnp.concatenate([pieces[y], pieces[N_Y + y]], axis=0).astype(jnp.bfloat16)
        out_ref[y] = pair
        out_ref[N_Y + y] = pair


def project(heads, more_heads, w_ot):
    cost = pl.CostEstimate(
        flops=2 * FEAT * HALF * TOKENS, bytes_accessed=2 * 2**20, transcendentals=0
    )
    first = pl.pallas_call(
        project_own_kernel,
        out_shape=shape(FEAT, TOKENS, dtype=jnp.float32),
        in_specs=[VMEM] * 2,
        out_specs=VMEM,
        compiler_params=params(),
        cost_estimate=cost,
        name="project_own",
    )(heads, w_ot)
    return pl.pallas_call(
        project_more_kernel,
        out_shape=shape(N_TP, PAIR, TOKENS),
        in_specs=[VMEM] * 3,
        out_specs=VMEM,
        compiler_params=params(),
        cost_estimate=cost,
        name="project_more",
    )(first, more_heads, w_ot)


def update_kernel(parts_ref, residual_ref, updated_ref, out_ref):
    attended = jnp.sum(parts_ref[...].astype(jnp.float32), axis=0)
    updated = (residual_ref[...].astype(jnp.float32) + attended).astype(jnp.bfloat16)
    updated_ref[...] = updated
    for i in range(N_RING):
        out_ref[i] = updated


def update(parts, residual):
    return pl.pallas_call(
        update_kernel,
        out_shape=(shape(PAIR, TOKENS), shape(N_RING, PAIR, TOKENS)),
        in_specs=[VMEM] * 2,
        out_specs=(VMEM, VMEM),
        compiler_params=params(),
        name="update",
    )(parts, residual)


def spaced(ref):
    wide = ref[...].astype(jnp.float32).reshape(SIDE, TOKENS)
    squares = jnp.sum(wide * wide, axis=0, keepdims=True)
    wide = jnp.concatenate([wide, jnp.zeros((8, TOKENS), jnp.float32)], axis=0)
    pieces = [wide[i * PIECE : i * PIECE + PAD] for i in range(SIDE // PIECE)]
    return jnp.concatenate(pieces, axis=0).astype(jnp.bfloat16), squares


def mix_own_kernel(own_ref, *refs):
    blocks, (out_ref, squares_ref, held, sems) = refs[:N_Y], refs[N_Y:]
    copies = [
        pltpu.make_async_copy(blocks[k].at[:, pl.ds(0, OUT)], held.at[k], sems.at[k])
        for k in range(N_Y)
    ]
    for copy in copies:
        copy.start()
    own, squares_ref[...] = spaced(own_ref)
    for k in range(N_Y):
        copies[k].wait()
        out_ref[k] = dot(held[k], own)


def mix_more_kernel(part_ref, squares_ref, more_ref, *refs):
    blocks, (out_ref, held, sems) = refs[:N_Y], refs[N_Y:]
    copies = [
        pltpu.make_async_copy(blocks[k].at[:, pl.ds(OUT, OUT)], held.at[k], sems.at[k])
        for k in range(N_Y)
    ]
    for copy in copies:
        copy.start()
    more, squares = spaced(more_ref)
    squares = squares_ref[...] + squares
    high = squares.astype(jnp.bfloat16).astype(jnp.float32)
    row = lax.broadcasted_iota(jnp.int32, (2 * ROOM, TOKENS), 0)
    y = lax.axis_index("y")
    for k in range(N_Y):
        copies[k].wait()
        part = part_ref[k] + dot(held[k], more)
        part = jnp.where(row == FF, high, jnp.where(row == FF + 1, squares - high, part))
        out_ref[y ^ k] = part.astype(jnp.bfloat16)


def mix(own, more, blocks):
    scratch = [
        pltpu.VMEM((N_Y, 2 * ROOM, OUT), jnp.bfloat16),
        pltpu.SemaphoreType.DMA((N_Y,)),
    ]
    cost = pl.CostEstimate(
        flops=2 * N_Y * 2 * ROOM * OUT * TOKENS, bytes_accessed=4 * 2**20, transcendentals=0
    )
    part, squares = pl.pallas_call(
        mix_own_kernel,
        out_shape=(
            shape(N_Y, 2 * ROOM, TOKENS, dtype=jnp.float32),
            shape(1, TOKENS, dtype=jnp.float32),
        ),
        in_specs=[VMEM] + [ANY] * N_Y,
        out_specs=(VMEM, VMEM),
        scratch_shapes=scratch,
        compiler_params=params(),
        cost_estimate=cost,
        name="mix_own",
    )(own, *blocks)
    return pl.pallas_call(
        mix_more_kernel,
        out_shape=shape(N_Y, 2 * ROOM, TOKENS),
        in_specs=[VMEM] * 3 + [ANY] * N_Y,
        out_specs=VMEM,
        scratch_shapes=scratch,
        compiler_params=params(),
        cost_estimate=cost,
        name="mix_more",
    )(part, squares, more, *blocks)


def gate_kernel(parts_ref, out_ref):
    total = jnp.sum(parts_ref[...].astype(jnp.float32), axis=0)
    mean = (total[FF : FF + 1] + total[FF + 1 : FF + 2]) * (1.0 / D)
    inverse_rms = lax.rsqrt(mean + EPS)
    gate_out, up_out = total[:ROOM] * inverse_rms, total[ROOM:] * inverse_rms
    row = lax.broadcasted_iota(jnp.int32, (ROOM, TOKENS), 0)
    hidden = jnp.where(row < FF, gate_out / (1.0 + jnp.exp(-gate_out)) * up_out, 0.0)
    hidden = hidden.astype(jnp.bfloat16)
    for t in range(N_Y):
        out_ref[t] = hidden


def gate(parts):
    return pl.pallas_call(
        gate_kernel,
        out_shape=shape(N_Y, ROOM, TOKENS),
        in_specs=[VMEM],
        out_specs=VMEM,
        compiler_params=params(),
        name="gate",
    )(parts)


def down_kernel(side, hidden_ref, *refs):
    blocks, (out_ref, held, hidden, sems) = refs[:N_Y], refs[N_Y:]
    copies = [
        pltpu.make_async_copy(
            blocks[k].at[:, pl.ds(side * OUT, OUT)], held.at[pl.ds(k * ROOM, ROOM), :], sems.at[k]
        )
        for k in range(N_Y)
    ]
    for copy in copies:
        copy.start()
    y = lax.axis_index("y")
    for k in range(N_Y):
        hidden[k * ROOM : (k + 1) * ROOM, :] = hidden_ref[y ^ k]
    for copy in copies:
        copy.wait()
    out_ref[...] = dot(held[...], hidden[...], TN).astype(out_ref.dtype)


def down(side, hidden, blocks):
    return pl.pallas_call(
        functools.partial(down_kernel, side),
        out_shape=shape(OUT, TOKENS, dtype=jnp.bfloat16 if side else jnp.float32),
        in_specs=[VMEM] + [ANY] * N_Y,
        out_specs=VMEM,
        scratch_shapes=[
            pltpu.VMEM((N_Y * ROOM, OUT), jnp.bfloat16),
            pltpu.VMEM((N_Y * ROOM, TOKENS), jnp.bfloat16),
            pltpu.SemaphoreType.DMA((N_Y,)),
        ],
        compiler_params=params(),
        cost_estimate=pl.CostEstimate(
            flops=2 * N_Y * ROOM * OUT * TOKENS, bytes_accessed=3 * 2**20, transcendentals=0
        ),
        name="down",
    )(hidden, *blocks)


def swap(x, axes):
    return lax.all_to_all(x, axes, 0, 0, tiled=True)


def other_core(x):
    return lax.ppermute(x, "c", [(0, 1), (1, 0)])


def other_half(x):
    return lax.ppermute(x, "xh", [(0, 1), (1, 0)])


def body(
    queries, new_latent, cache, cache_lengths, w_uv, w_o, residual, norm_gain, w_gate, w_up, w_down
):
    xh = lax.axis_index("xh")

    mine, theirs = attend(
        cache_lengths.T, queries.reshape(ROWS, KDIM), jnp.transpose(new_latent, (1, 0, 2)), cache.T,
        w_uv,
    )

    def exchange(block, k):
        return lax.ppermute(block, "y", [(i, i ^ k) for i in range(N_Y)])

    gain = norm_gain.reshape(D // 128, 128)
    sources = (w_gate.T, w_up.T)
    mix_1, mix_3 = regroup((1, 3), sources, gain, True, mine)
    mix_2, mix_0 = regroup((2, 0), sources, gain, True, mix_1)

    heads = swap(fan(mine, other_core(theirs)), RING).reshape(TOKENS, HALF)
    heads, mix_1, mix_3, mix_0 = lax.optimization_barrier(
        (heads, exchange(mix_1, 1), exchange(mix_3, 3), mix_0)
    )
    partial = project(heads, other_core(heads), w_o.T)

    partner = other_half(residual.T)
    residual = jnp.concatenate(
        [jnp.where(xh == 0, residual.T, partner), jnp.where(xh == 0, partner, residual.T)], axis=0
    )
    down_blocks = regroup((1, 3, 2, 0), (w_down,), gain, False, partial)
    updated, block = update(swap(partial, TP), residual)
    block, mix_2, *down_blocks = lax.optimization_barrier(
        (block, exchange(mix_2, 2), *down_blocks)
    )
    down_1, down_3, down_2, down_0 = down_blocks
    own, down_1, down_2, down_3 = lax.optimization_barrier(
        (swap(block, RING), exchange(down_1, 1), exchange(down_2, 2), exchange(down_3, 3))
    )
    mix_blocks, down_blocks = (mix_0, mix_1, mix_2, mix_3), (down_0, down_1, down_2, down_3)
    hidden = gate(swap(mix(own, other_core(own), mix_blocks), "y"))
    hidden = swap(hidden, "y")
    more = other_core(down(1, hidden, down_blocks))
    term = down(0, hidden, down_blocks) + more.astype(jnp.float32)
    term = swap(term.astype(jnp.bfloat16).reshape(2 * N_RING, PAD, TOKENS), RING + ("xh",))
    term = jnp.sum(term.astype(jnp.float32), axis=0)[:PIECE]
    updated = jnp.where(xh == 0, updated[:PIECE], updated[PIECE:])
    return (updated.astype(jnp.float32) + term).astype(jnp.bfloat16).T


def solution(mesh):
    parts = Mesh(mesh.devices.reshape(tuple(SIZES.values())), tuple(SIZES))
    everywhere = DP + TP
    return jax.shard_map(
        body,
        mesh=parts,
        in_specs=(
            P(DP, None, TP, None),
            P(DP, None, None),
            P(DP, None),
            P(),
            P(TP, None, None),
            P(TP, DP),
            P(None, everywhere),
            P(),
            P(None, everywhere),
            P(None, everywhere),
            P(everywhere, None),
        ),
        out_specs=P(None, everywhere),
        check_vma=False,
    )
```

```python
import functools

import jax
import jax.numpy as jnp
from jax import lax
from jax.experimental import pallas as pl
from jax.experimental.pallas import tpu as pltpu
from jax.sharding import Mesh, PartitionSpec as P

DP = ("xl", "z", "c")
RING = ("xl", "z")
TP = ("xh", "y")
SIZES = {"xl": 2, "z": 8, "c": 2, "xh": 2, "y": 4}
N_RING, N_TP, N_Y = 16, 8, 4

STEPS, HEADS, REQ = 3, 16, 4
NEW = REQ * STEPS
ROWS = NEW * HEADS
TOKENS = 384
LAT, KDIM, VDIM = 512, 576, 128
HALF = HEADS // 2 * VDIM
CTX, CHUNK = 4096, 1024
N_CHUNK = CTX // CHUNK
D, FEAT, PIECE, PAD = 7168, 224, 28, 32
PAIR = 2 * PIECE
SIDE = N_RING * PAIR
OUT = N_RING * 2 * PAD
FF, ROOM = 72, 80
EPS = 1e-06
LOG2E = 1.4426950408889634
SCALE = 192.0 ** (-0.5)
NEG = -1e30

NT = (((1,), (1,)), ((), ()))
TN = (((0,), (0,)), ((), ()))

VMEM = pl.BlockSpec(memory_space=pltpu.VMEM)
SMEM = pl.BlockSpec(memory_space=pltpu.SMEM)
ANY = pl.BlockSpec(memory_space=pl.ANY)
HBM = pl.BlockSpec(memory_space=pltpu.HBM)


def params(mib=12):
    return pltpu.CompilerParams(vmem_limit_bytes=mib * 2**20)


def shape(*dims, dtype=jnp.bfloat16):
    return jax.ShapeDtypeStruct(dims, dtype)


def dot(a, b, dims=(((1,), (0,)), ((), ()))):
    return lax.dot_general(a, b, dims, preferred_element_type=jnp.float32)


def attend_kernel(
    lengths, q_ref, fresh_ref, cache_hbm, w_uv_hbm, out_ref, keys, scores, w_uv,
    new_keys, key_sems, w_sem,
):
    copies = [
        pltpu.make_async_copy(
            cache_hbm.at[:, pl.ds(j * CHUNK, CHUNK)], keys.at[j], key_sems.at[j]
        )
        for j in range(N_CHUNK)
    ]
    w_copy = pltpu.make_async_copy(w_uv_hbm, w_uv, w_sem)
    for copy in copies:
        copy.start()

    dp_index = lax.axis_index(DP)
    q = q_ref[...]
    row = lax.broadcasted_iota(jnp.int32, (ROWS, 1), 0)
    request = row // (STEPS * HEADS)
    step = row // HEADS - request * STEPS
    low = jnp.zeros((ROWS, 1), jnp.int32)
    high = jnp.zeros((ROWS, 1), jnp.int32)
    start = 0
    for r in range(REQ):
        end = start + lengths[r, dp_index]
        low = jnp.where(request == r, start, low)
        high = jnp.where(request == r, end, high)
        start = end

    new_keys[...] = jnp.zeros_like(new_keys)
    for i in range(STEPS):
        new_keys[i * REQ : (i + 1) * REQ, :] = fresh_ref[i].astype(jnp.float32)
    fresh = new_keys[...].astype(jnp.bfloat16)
    key = lax.broadcasted_iota(jnp.int32, (ROWS, 16), 1)
    key_step = key // REQ
    seen = (key - key_step * REQ == request) & (key_step <= step)
    fresh_scores = jnp.where(seen, dot(q, fresh, NT) * (SCALE * LOG2E), NEG)
    top = jnp.max(fresh_scores, axis=1, keepdims=True)

    tops = jnp.full((ROWS, 128), NEG, jnp.float32)
    for j in range(N_CHUNK):
        copies[j].wait()
        if j == 1:
            w_copy.start()
        slot = j * CHUNK + lax.broadcasted_iota(jnp.int32, (ROWS, CHUNK), 1)
        part = dot(q, keys[j]) * (SCALE * LOG2E)
        part = jnp.where((slot >= low) & (slot < high), part, NEG)
        scores[j] = part
        for i in range(0, CHUNK, 128):
            tops = jnp.maximum(tops, part[:, i : i + 128])
    top = jnp.maximum(top, jnp.max(tops, axis=1, keepdims=True))

    totals = jnp.zeros((ROWS, 128), jnp.float32)
    weights = jnp.exp2(fresh_scores - top)
    total = jnp.sum(weights, axis=1, keepdims=True)
    mixed = dot(weights.astype(jnp.bfloat16), fresh[:, :LAT])
    for j in range(N_CHUNK):
        weights = jnp.exp2(scores[j] - top)
        for i in range(0, CHUNK, 128):
            totals = totals + weights[:, i : i + 128]
        mixed = mixed + dot(weights.astype(jnp.bfloat16), keys[j, :LAT, :], NT)
    total = total + jnp.sum(totals, axis=1, keepdims=True)
    mixed = (mixed / total).astype(jnp.bfloat16)

    w_copy.wait()
    head = row - (row // HEADS) * HEADS
    halves = []
    for half in range(2):
        values = []
        for h in range(half * HEADS // 2, (half + 1) * HEADS // 2, 2):
            pair = dot(mixed, jnp.concatenate([w_uv[h], w_uv[h + 1]], axis=1))
            for i in range(2):
                value = jnp.where(head == h + i, pair[:, i * VDIM : (i + 1) * VDIM], 0.0)
                values.append(jnp.sum(value.reshape(NEW, HEADS, VDIM), axis=1))
        halves.append(jnp.concatenate(values, axis=1))
    both = jnp.concatenate(halves, axis=0).astype(jnp.bfloat16)
    for i in range(N_RING):
        out_ref[i] = both


def attend(lengths, q, fresh, cache_t, w_uv):
    return pl.pallas_call(
        attend_kernel,
        out_shape=shape(N_RING, 2 * NEW, HALF),
        in_specs=[SMEM, VMEM, VMEM, ANY, ANY],
        out_specs=VMEM,
        scratch_shapes=[
            pltpu.VMEM((N_CHUNK, KDIM, CHUNK), jnp.bfloat16),
            pltpu.VMEM((N_CHUNK, ROWS, CHUNK), jnp.float32),
            pltpu.VMEM((HEADS, LAT, VDIM), jnp.bfloat16),
            pltpu.VMEM((16, KDIM), jnp.float32),
            pltpu.SemaphoreType.DMA((N_CHUNK,)),
            pltpu.SemaphoreType.DMA,
        ],
        compiler_params=params(58),
        cost_estimate=pl.CostEstimate(
            flops=2 * ROWS * CTX * (KDIM + LAT), bytes_accessed=7 * 2**20, transcendentals=ROWS * CTX
        ),
        name="attend",
    )(lengths, q, fresh, cache_t, w_uv)


def one_hot(rows, columns, source):
    column = lax.broadcasted_iota(jnp.int32, (1, columns), 1)
    row = lax.broadcasted_iota(jnp.int32, (rows, columns), 0)
    return jnp.where(row == source(column), 1.0, 0.0).astype(jnp.bfloat16)


def token_order():
    def source(at):
        core, rest = at // (N_RING * NEW), at % (N_RING * NEW)
        return (rest // NEW * 2 + core) * NEW + rest % NEW

    return one_hot(TOKENS, TOKENS, source)


def pick_columns(ks, width):
    lanes = len(ks) * 8 * PAD
    lane = lax.broadcasted_iota(jnp.int32, (1, lanes), 1)
    n, side, u = lane // (8 * PAD), lane // (4 * PAD) % 2, lane // (2 * PAD) % 2
    k = jnp.zeros_like(n)
    for i in range(len(ks)):
        k = jnp.where(n == i, ks[i], k)
    xh, j = lane // PAD % 2, lane % PAD
    source = (2 * u + (side ^ lax.axis_index("c"))) * FEAT
    source = source + (xh * N_Y + (k ^ lax.axis_index("y"))) * PIECE + j
    source = jnp.where(j < PIECE, source, -1)
    rows = lax.broadcasted_iota(jnp.int32, (width, lanes), 0)
    return jnp.where(rows == source, 1.0, 0.0).astype(jnp.bfloat16)


def regroup_kernel(ks, count, *refs):
    sources, gain_ref, refs = refs[:count], refs[count], refs[count + 2 :]
    outs, (rows, loaded, moved_ref, in_sems, out_sems) = refs[:-5], refs[-5:]
    width = 4 * FEAT
    loads = [
        pltpu.make_async_copy(source, loaded.at[i], in_sems.at[i])
        for i, source in enumerate(sources)
    ]
    for load in loads:
        load.start()
    pick = pick_columns(ks, width)
    for load in loads:
        load.wait()
    if count == 2:
        for j in range(D // 128):
            lanes = slice(j * 128, (j + 1) * 128)
            both = [loaded[i, :, lanes].astype(jnp.float32) for i in range(count)]
            both = jnp.concatenate(both, axis=0) * gain_ref[j : j + 1, :].astype(jnp.float32)
            rows[:, lanes] = both.astype(jnp.bfloat16)
    else:
        rows[ROOM - 16 :, :] = jnp.zeros((16, D), jnp.bfloat16)
        rows[:FF, :] = loaded[0]
    stores = []
    for n in range(len(ks)):
        for m in range(D // width):
            moved = dot(rows[:, m * width : (m + 1) * width], pick[:, n * 256 : (n + 1) * 256])
            moved = moved.astype(jnp.bfloat16)
            for side in range(2):
                to = (side * 8 + m) * 128
                moved_ref[n, :, to : to + 128] = moved[:, side * 128 : (side + 1) * 128]
        stores.append(pltpu.make_async_copy(moved_ref.at[n], outs[n], out_sems.at[n]))
        stores[-1].start()
    for store in stores:
        store.wait()


def regroup(ks, sources, gain, after):
    count = len(sources)
    height = 2 * FF if count == 2 else ROOM
    return pl.pallas_call(
        functools.partial(regroup_kernel, ks, count),
        out_shape=[shape(height, 2 * OUT)] * len(ks),
        in_specs=[HBM] * count + [VMEM, ANY],
        out_specs=[HBM] * len(ks),
        scratch_shapes=[
            pltpu.VMEM((height, D), jnp.bfloat16),
            pltpu.VMEM((count, FF, D), jnp.bfloat16),
            pltpu.VMEM((len(ks), height, 2 * OUT), jnp.bfloat16),
            pltpu.SemaphoreType.DMA((count,)),
            pltpu.SemaphoreType.DMA((len(ks),)),
        ],
        compiler_params=params(58),
        cost_estimate=pl.CostEstimate(
            flops=2 * height * D * 256 * len(ks), bytes_accessed=5 * 2**20, transcendentals=0
        ),
        name="regroup",
    )(*sources, gain, after)


def project_heads(heads_ref, w_ref):
    def source(at):
        ring, rest = at // (2 * NEW), at % (2 * NEW)
        return rest // NEW * (N_RING * NEW) + ring * NEW + rest % NEW

    split = one_hot(TOKENS, TOKENS, source)
    heads = dot(split, heads_ref[...]).astype(jnp.bfloat16)
    return dot(w_ref[:, :HALF], heads[: N_RING * NEW], NT) + dot(
        w_ref[:, HALF:], heads[N_RING * NEW :], NT
    )


def project_own_kernel(heads_ref, w_ref, out_ref):
    out_ref[...] = project_heads(heads_ref, w_ref).astype(jnp.bfloat16)


def project_more_kernel(first_ref, heads_ref, w_ref, out_ref):
    more = project_heads(heads_ref, w_ref).astype(jnp.bfloat16)
    core, count = lax.axis_index("c"), N_RING * NEW
    own_place = one_hot(count, TOKENS, lambda at: at - core * count)
    more_place = one_hot(count, TOKENS, lambda at: at - (1 - core) * count)
    total = dot(first_ref[...], own_place) + dot(more, more_place)

    def source(at):
        t, j = at // PIECE, at % PIECE
        return (t % N_Y * 2 + t // N_Y) * PIECE + j

    total = dot(one_hot(FEAT, FEAT, source), total.astype(jnp.bfloat16))
    for y in range(N_Y):
        pair = total[y * PAIR : (y + 1) * PAIR].astype(jnp.bfloat16)
        out_ref[y] = pair
        out_ref[N_Y + y] = pair


def project(heads, more_heads, w_ot):
    cost = pl.CostEstimate(
        flops=2 * FEAT * HALF * TOKENS, bytes_accessed=2 * 2**20, transcendentals=0
    )
    first = pl.pallas_call(
        project_own_kernel,
        out_shape=shape(FEAT, N_RING * NEW),
        in_specs=[VMEM] * 2,
        out_specs=VMEM,
        compiler_params=params(),
        cost_estimate=cost,
        name="project_own",
    )(heads, w_ot)
    return pl.pallas_call(
        project_more_kernel,
        out_shape=shape(N_TP, PAIR, TOKENS),
        in_specs=[VMEM] * 3,
        out_specs=VMEM,
        compiler_params=params(),
        cost_estimate=cost,
        name="project_more",
    )(first, more_heads, w_ot)


def update_kernel(parts_ref, residual_ref, updated_ref, out_ref):
    attended = jnp.sum(parts_ref[...].astype(jnp.float32), axis=0)
    updated = (dot(residual_ref[...], token_order()) + attended).astype(jnp.bfloat16)
    updated_ref[...] = updated
    for i in range(N_RING):
        out_ref[i] = updated


def update(parts, residual):
    return pl.pallas_call(
        update_kernel,
        out_shape=(shape(PAIR, TOKENS), shape(N_RING, PAIR, TOKENS)),
        in_specs=[VMEM] * 2,
        out_specs=(VMEM, VMEM),
        compiler_params=params(),
        name="update",
    )(parts, residual)


def spaced(ref):
    wide = ref[...].astype(jnp.float32).reshape(SIDE, TOKENS)
    squares = jnp.sum(wide * wide, axis=0, keepdims=True)
    wide = jnp.concatenate([wide, jnp.zeros((8, TOKENS), jnp.float32)], axis=0)
    pieces = [wide[i * PIECE : i * PIECE + PAD] for i in range(SIDE // PIECE)]
    return jnp.concatenate(pieces, axis=0).astype(jnp.bfloat16), squares


def mix_own_kernel(own_ref, *refs):
    blocks, (out_ref, squares_ref, held, sems) = refs[:N_Y], refs[N_Y:]
    copies = [
        pltpu.make_async_copy(blocks[k].at[:, pl.ds(0, OUT)], held.at[k], sems.at[k])
        for k in range(N_Y)
    ]
    for copy in copies:
        copy.start()
    own, squares_ref[...] = spaced(own_ref)
    for k in range(N_Y):
        copies[k].wait()
        out_ref[k] = dot(held[k], own)


def mix_more_kernel(part_ref, squares_ref, more_ref, *refs):
    blocks, (out_ref, held, sems) = refs[:N_Y], refs[N_Y:]
    copies = [
        pltpu.make_async_copy(blocks[k].at[:, pl.ds(OUT, OUT)], held.at[k], sems.at[k])
        for k in range(N_Y)
    ]
    for copy in copies:
        copy.start()
    more, squares = spaced(more_ref)
    squares = squares_ref[...] + squares
    high = squares.astype(jnp.bfloat16).astype(jnp.float32)
    row = lax.broadcasted_iota(jnp.int32, (16, TOKENS), 0)
    tail = jnp.where(row == 0, high, jnp.where(row == 1, squares - high, 0.0))
    tail = tail.astype(jnp.bfloat16)
    y = lax.axis_index("y")
    for k in range(N_Y):
        copies[k].wait()
        part = part_ref[k] + dot(held[k], more)
        out_ref[y ^ k, : 2 * FF, :] = part.astype(jnp.bfloat16)
        out_ref[y ^ k, 2 * FF :, :] = tail


def mix(own, more, blocks):
    scratch = [
        pltpu.VMEM((N_Y, 2 * FF, OUT), jnp.bfloat16),
        pltpu.SemaphoreType.DMA((N_Y,)),
    ]
    cost = pl.CostEstimate(
        flops=2 * N_Y * 2 * FF * OUT * TOKENS, bytes_accessed=4 * 2**20, transcendentals=0
    )
    part, squares = pl.pallas_call(
        mix_own_kernel,
        out_shape=(
            shape(N_Y, 2 * FF, TOKENS, dtype=jnp.float32),
            shape(1, TOKENS, dtype=jnp.float32),
        ),
        in_specs=[VMEM] + [ANY] * N_Y,
        out_specs=(VMEM, VMEM),
        scratch_shapes=scratch,
        compiler_params=params(),
        cost_estimate=cost,
        name="mix_own",
    )(own, *blocks)
    return pl.pallas_call(
        mix_more_kernel,
        out_shape=shape(N_Y, 2 * FF + 16, TOKENS),
        in_specs=[VMEM] * 3 + [ANY] * N_Y,
        out_specs=VMEM,
        scratch_shapes=scratch,
        compiler_params=params(),
        cost_estimate=cost,
        name="mix_more",
    )(part, squares, more, *blocks)


def gate_kernel(parts_ref, out_ref):
    total = jnp.sum(parts_ref[...].astype(jnp.float32), axis=0)
    mean = (total[2 * FF : 2 * FF + 1] + total[2 * FF + 1 : 2 * FF + 2]) * (1.0 / D)
    inverse_rms = lax.rsqrt(mean + EPS)
    gate_out, up_out = total[:FF] * inverse_rms, total[FF : 2 * FF] * inverse_rms
    hidden = gate_out / (1.0 + jnp.exp(-gate_out)) * up_out
    hidden = jnp.concatenate([hidden, jnp.zeros((ROOM - FF, TOKENS), jnp.float32)], axis=0)
    hidden = hidden.astype(jnp.bfloat16)
    for t in range(N_Y):
        out_ref[t] = hidden


def gate(parts):
    return pl.pallas_call(
        gate_kernel,
        out_shape=shape(N_Y, ROOM, TOKENS),
        in_specs=[VMEM],
        out_specs=VMEM,
        compiler_params=params(),
        name="gate",
    )(parts)


def down_kernel(side, hidden_ref, *refs):
    blocks, (out_ref, held, hidden, sems) = refs[:N_Y], refs[N_Y:]
    copies = [
        pltpu.make_async_copy(
            blocks[k].at[:, pl.ds(side * OUT, OUT)], held.at[pl.ds(k * ROOM, ROOM), :], sems.at[k]
        )
        for k in range(N_Y)
    ]
    for copy in copies:
        copy.start()
    y = lax.axis_index("y")
    for k in range(N_Y):
        hidden[k * ROOM : (k + 1) * ROOM, :] = hidden_ref[y ^ k]
    for copy in copies:
        copy.wait()
    out_ref[...] = dot(held[...], hidden[...], TN).astype(out_ref.dtype)


def down(side, hidden, blocks):
    return pl.pallas_call(
        functools.partial(down_kernel, side),
        out_shape=shape(OUT, TOKENS, dtype=jnp.bfloat16 if side else jnp.float32),
        in_specs=[VMEM] + [ANY] * N_Y,
        out_specs=VMEM,
        scratch_shapes=[
            pltpu.VMEM((N_Y * ROOM, OUT), jnp.bfloat16),
            pltpu.VMEM((N_Y * ROOM, TOKENS), jnp.bfloat16),
            pltpu.SemaphoreType.DMA((N_Y,)),
        ],
        compiler_params=params(),
        cost_estimate=pl.CostEstimate(
            flops=2 * N_Y * ROOM * OUT * TOKENS, bytes_accessed=3 * 2**20, transcendentals=0
        ),
        name="down",
    )(hidden, *blocks)


def finish_kernel(updated_ref, parts_ref, out_ref):
    wide = updated_ref[...].astype(jnp.float32)
    own = jnp.where(lax.axis_index("xh") == 0, wide[:PIECE], wide[PIECE:])
    total = own + jnp.sum(parts_ref[...].astype(jnp.float32), axis=0)[:PIECE]
    out_ref[...] = dot(total.astype(jnp.bfloat16), token_order(), NT).astype(jnp.bfloat16)


def finish(updated, parts):
    return pl.pallas_call(
        finish_kernel,
        out_shape=shape(PIECE, TOKENS),
        in_specs=[VMEM] * 2,
        out_specs=VMEM,
        compiler_params=params(),
        name="finish",
    )(updated, parts)


def swap(x, axes):
    return lax.all_to_all(x, axes, 0, 0, tiled=True)


def other_core(x):
    return lax.ppermute(x, "c", [(0, 1), (1, 0)])


def other_half(x):
    return lax.ppermute(x, "xh", [(0, 1), (1, 0)])


def body(
    queries, new_latent, cache, cache_lengths, w_uv, w_o, residual, norm_gain, w_gate, w_up, w_down
):
    xh = lax.axis_index("xh")

    heads = attend(
        cache_lengths.T, queries.reshape(ROWS, KDIM), jnp.transpose(new_latent, (1, 0, 2)), cache.T,
        w_uv,
    )

    def exchange(block, k):
        return lax.ppermute(block, "y", [(i, i ^ k) for i in range(N_Y)])

    gain = norm_gain.reshape(D // 128, 128)
    sources = (w_gate.T, w_up.T)
    mix_1, mix_3 = regroup((1, 3), sources, gain, heads)
    mix_2, mix_0 = regroup((2, 0), sources, gain, mix_1)

    heads = swap(heads, RING).reshape(TOKENS, HALF)
    heads, mix_1, mix_3, mix_0 = lax.optimization_barrier(
        (heads, exchange(mix_1, 1), exchange(mix_3, 3), mix_0)
    )
    partial = project(heads, other_core(heads), w_o.T)

    partner = other_half(residual.T)
    residual = jnp.concatenate(
        [jnp.where(xh == 0, residual.T, partner), jnp.where(xh == 0, partner, residual.T)], axis=0
    )
    down_blocks = regroup((1, 3, 2, 0), (w_down,), gain, partial)
    parts, mix_2, *down_blocks = lax.optimization_barrier(
        (swap(partial, TP), exchange(mix_2, 2), *down_blocks)
    )
    updated, block = update(parts, residual)
    down_1, down_3, down_2, down_0 = down_blocks
    own, down_1, down_2, down_3 = lax.optimization_barrier(
        (swap(block, RING), exchange(down_1, 1), exchange(down_2, 2), exchange(down_3, 3))
    )
    mix_blocks, down_blocks = (mix_0, mix_1, mix_2, mix_3), (down_0, down_1, down_2, down_3)
    hidden = gate(swap(mix(own, other_core(own), mix_blocks), "y"))
    hidden = swap(hidden, "y")
    more = other_core(down(1, hidden, down_blocks))
    term = down(0, hidden, down_blocks) + more.astype(jnp.float32)
    term = swap(term.astype(jnp.bfloat16).reshape(2 * N_RING, PAD, TOKENS), RING + ("xh",))
    return finish(updated, term).T


def solution(mesh):
    parts = Mesh(mesh.devices.reshape(tuple(SIZES.values())), tuple(SIZES))
    everywhere = DP + TP
    return jax.shard_map(
        body,
        mesh=parts,
        in_specs=(
            P(DP, None, TP, None),
            P(DP, None, None),
            P(DP, None),
            P(),
            P(TP, None, None),
            P(TP, DP),
            P(None, everywhere),
            P(),
            P(None, everywhere),
            P(None, everywhere),
            P(everywhere, None),
        ),
        out_specs=P(None, everywhere),
        check_vma=False,
    )
```

```python
import functools

import jax
import jax.numpy as jnp
from jax import lax
from jax.experimental import pallas as pl
from jax.experimental.pallas import tpu as pltpu
from jax.sharding import Mesh, PartitionSpec as P

DP = ("xl", "z", "c")
RING = ("xl", "z")
TP = ("xh", "y")
SIZES = {"xl": 2, "z": 8, "c": 2, "xh": 2, "y": 4}
N_RING, N_TP, N_Y = 16, 8, 4

STEPS, HEADS, REQ = 3, 16, 4
NEW = REQ * STEPS
ROWS = NEW * HEADS
TOKENS = 384
LAT, KDIM, VDIM = 512, 576, 128
HALF = HEADS // 2 * VDIM
CTX, CHUNK = 4096, 1024
N_CHUNK = CTX // CHUNK
D, FEAT, PIECE, PAD = 7168, 224, 28, 32
PAIR = 2 * PIECE
SIDE = N_RING * PAIR
OUT = N_RING * 2 * PAD
FF, ROOM = 72, 80
EPS = 1e-06
LOG2E = 1.4426950408889634
SCALE = 192.0 ** (-0.5)
NEG = -1e30

NT = (((1,), (1,)), ((), ()))
TN = (((0,), (0,)), ((), ()))

VMEM = pl.BlockSpec(memory_space=pltpu.VMEM)
SMEM = pl.BlockSpec(memory_space=pltpu.SMEM)
ANY = pl.BlockSpec(memory_space=pl.ANY)
HBM = pl.BlockSpec(memory_space=pltpu.HBM)


def params(mib=12):
    return pltpu.CompilerParams(vmem_limit_bytes=mib * 2**20)


def shape(*dims, dtype=jnp.bfloat16):
    return jax.ShapeDtypeStruct(dims, dtype)


def dot(a, b, dims=(((1,), (0,)), ((), ()))):
    return lax.dot_general(a, b, dims, preferred_element_type=jnp.float32)


def attend_kernel(
    lengths, q_ref, fresh_ref, cache_hbm, w_uv_hbm, out_ref, keys, scores, w_uv,
    new_keys, key_sems, w_sem,
):
    copies = [
        pltpu.make_async_copy(
            cache_hbm.at[:, pl.ds(j * CHUNK, CHUNK)], keys.at[j], key_sems.at[j]
        )
        for j in range(N_CHUNK)
    ]
    w_copy = pltpu.make_async_copy(w_uv_hbm, w_uv, w_sem)
    for copy in copies:
        copy.start()

    dp_index = lax.axis_index(DP)
    q = q_ref[...]
    row = lax.broadcasted_iota(jnp.int32, (ROWS, 1), 0)
    request = row // (STEPS * HEADS)
    step = row // HEADS - request * STEPS
    low = jnp.zeros((ROWS, 1), jnp.int32)
    high = jnp.zeros((ROWS, 1), jnp.int32)
    start = 0
    for r in range(REQ):
        end = start + lengths[r, dp_index]
        low = jnp.where(request == r, start, low)
        high = jnp.where(request == r, end, high)
        start = end

    new_keys[...] = jnp.zeros_like(new_keys)
    for i in range(STEPS):
        new_keys[i * REQ : (i + 1) * REQ, :] = fresh_ref[i].astype(jnp.float32)
    fresh = new_keys[...].astype(jnp.bfloat16)
    key = lax.broadcasted_iota(jnp.int32, (ROWS, 16), 1)
    key_step = key // REQ
    seen = (key - key_step * REQ == request) & (key_step <= step)
    fresh_scores = jnp.where(seen, dot(q, fresh, NT) * (SCALE * LOG2E), NEG)
    top = jnp.max(fresh_scores, axis=1, keepdims=True)

    tops = jnp.full((ROWS, 128), NEG, jnp.float32)
    for j in range(N_CHUNK):
        copies[j].wait()
        if j == 1:
            w_copy.start()
        slot = j * CHUNK + lax.broadcasted_iota(jnp.int32, (ROWS, CHUNK), 1)
        part = dot(q, keys[j]) * (SCALE * LOG2E)
        part = jnp.where((slot >= low) & (slot < high), part, NEG)
        scores[j] = part
        for i in range(0, CHUNK, 128):
            tops = jnp.maximum(tops, part[:, i : i + 128])
    top = jnp.maximum(top, jnp.max(tops, axis=1, keepdims=True))

    totals = jnp.zeros((ROWS, 128), jnp.float32)
    weights = jnp.exp2(fresh_scores - top)
    total = jnp.sum(weights, axis=1, keepdims=True)
    mixed = dot(weights.astype(jnp.bfloat16), fresh[:, :LAT])
    for j in range(N_CHUNK):
        weights = jnp.exp2(scores[j] - top)
        for i in range(0, CHUNK, 128):
            totals = totals + weights[:, i : i + 128]
        mixed = mixed + dot(weights.astype(jnp.bfloat16), keys[j, :LAT, :], NT)
    total = total + jnp.sum(totals, axis=1, keepdims=True)
    mixed = (mixed / total).astype(jnp.bfloat16)

    w_copy.wait()
    head = row - (row // HEADS) * HEADS
    halves = []
    for half in range(2):
        values = []
        for h in range(half * HEADS // 2, (half + 1) * HEADS // 2, 2):
            pair = dot(mixed, jnp.concatenate([w_uv[h], w_uv[h + 1]], axis=1))
            for i in range(2):
                value = jnp.where(head == h + i, pair[:, i * VDIM : (i + 1) * VDIM], 0.0)
                values.append(jnp.sum(value.reshape(NEW, HEADS, VDIM), axis=1))
        halves.append(jnp.concatenate(values, axis=1))
    both = jnp.concatenate(halves, axis=0).astype(jnp.bfloat16)
    for i in range(N_RING):
        out_ref[i] = both


def attend(lengths, q, fresh, cache_t, w_uv):
    return pl.pallas_call(
        attend_kernel,
        out_shape=shape(N_RING, 2 * NEW, HALF),
        in_specs=[SMEM, VMEM, VMEM, ANY, ANY],
        out_specs=VMEM,
        scratch_shapes=[
            pltpu.VMEM((N_CHUNK, KDIM, CHUNK), jnp.bfloat16),
            pltpu.VMEM((N_CHUNK, ROWS, CHUNK), jnp.float32),
            pltpu.VMEM((HEADS, LAT, VDIM), jnp.bfloat16),
            pltpu.VMEM((16, KDIM), jnp.float32),
            pltpu.SemaphoreType.DMA((N_CHUNK,)),
            pltpu.SemaphoreType.DMA,
        ],
        compiler_params=params(58),
        cost_estimate=pl.CostEstimate(
            flops=2 * ROWS * CTX * (KDIM + LAT), bytes_accessed=7 * 2**20, transcendentals=ROWS * CTX
        ),
        name="attend",
    )(lengths, q, fresh, cache_t, w_uv)


def one_hot(rows, columns, source):
    column = lax.broadcasted_iota(jnp.int32, (1, columns), 1)
    row = lax.broadcasted_iota(jnp.int32, (rows, columns), 0)
    return jnp.where(row == source(column), 1.0, 0.0).astype(jnp.bfloat16)


def token_order():
    def source(at):
        core, rest = at // (N_RING * NEW), at % (N_RING * NEW)
        return (rest // NEW * 2 + core) * NEW + rest % NEW

    return one_hot(TOKENS, TOKENS, source)


def pick_columns(ks, width):
    lanes = len(ks) * 8 * PAD
    lane = lax.broadcasted_iota(jnp.int32, (1, lanes), 1)
    n, side, u = lane // (8 * PAD), lane // (4 * PAD) % 2, lane // (2 * PAD) % 2
    k = jnp.zeros_like(n)
    for i in range(len(ks)):
        k = jnp.where(n == i, ks[i], k)
    xh, j = lane // PAD % 2, lane % PAD
    source = (2 * u + (side ^ lax.axis_index("c"))) * FEAT
    source = source + (xh * N_Y + (k ^ lax.axis_index("y"))) * PIECE + j
    source = jnp.where(j < PIECE, source, -1)
    rows = lax.broadcasted_iota(jnp.int32, (width, lanes), 0)
    return jnp.where(rows == source, 1.0, 0.0).astype(jnp.bfloat16)


def regroup_kernel(ks, count, *refs):
    sources, gain_ref, refs = refs[:count], refs[count], refs[count + 2 :]
    outs, (rows, moved_ref, out_sems) = refs[:-3], refs[-3:]
    width = 4 * FEAT
    pick = pick_columns(ks, width)
    for j in range(D // 128):
        lanes = slice(j * 128, (j + 1) * 128)
        wide = [ref[:, lanes].astype(jnp.float32) for ref in sources]
        if count == 2:
            wide = jnp.concatenate(wide, axis=0) * gain_ref[j : j + 1, :].astype(jnp.float32)
        else:
            wide = jnp.concatenate(wide + [jnp.zeros((ROOM - FF, 128), jnp.float32)], axis=0)
        rows[:, lanes] = wide.astype(jnp.bfloat16)
    stores = []
    for n in range(len(ks)):
        for m in range(D // width):
            moved = dot(rows[:, m * width : (m + 1) * width], pick[:, n * 256 : (n + 1) * 256])
            moved = moved.astype(jnp.bfloat16)
            for side in range(2):
                to = (side * 8 + m) * 128
                moved_ref[n, :, to : to + 128] = moved[:, side * 128 : (side + 1) * 128]
        stores.append(pltpu.make_async_copy(moved_ref.at[n], outs[n], out_sems.at[n]))
        stores[-1].start()
    for store in stores:
        store.wait()


def regroup(ks, sources, gain, after):
    count = len(sources)
    height = 2 * FF if count == 2 else ROOM
    return pl.pallas_call(
        functools.partial(regroup_kernel, ks, count),
        out_shape=[shape(height, 2 * OUT)] * len(ks),
        in_specs=[VMEM] * (count + 1) + [ANY],
        out_specs=[HBM] * len(ks),
        scratch_shapes=[
            pltpu.VMEM((height, D), jnp.bfloat16),
            pltpu.VMEM((len(ks), height, 2 * OUT), jnp.bfloat16),
            pltpu.SemaphoreType.DMA((len(ks),)),
        ],
        compiler_params=params(58),
        cost_estimate=pl.CostEstimate(
            flops=2 * height * D * 256 * len(ks), bytes_accessed=5 * 2**20, transcendentals=0
        ),
        name="regroup",
    )(*sources, gain, after)


def project_heads(heads_ref, w_ref):
    def source(at):
        ring, rest = at // (2 * NEW), at % (2 * NEW)
        return rest // NEW * (N_RING * NEW) + ring * NEW + rest % NEW

    split = one_hot(TOKENS, TOKENS, source)
    heads = dot(split, heads_ref[...]).astype(jnp.bfloat16)
    return dot(w_ref[:, :HALF], heads[: N_RING * NEW], NT) + dot(
        w_ref[:, HALF:], heads[N_RING * NEW :], NT
    )


def project_own_kernel(heads_ref, w_ref, out_ref):
    out_ref[...] = project_heads(heads_ref, w_ref).astype(jnp.bfloat16)


def project_more_kernel(first_ref, heads_ref, w_ref, out_ref):
    more = project_heads(heads_ref, w_ref).astype(jnp.bfloat16)
    core, count = lax.axis_index("c"), N_RING * NEW
    own_place = one_hot(count, TOKENS, lambda at: at - core * count)
    more_place = one_hot(count, TOKENS, lambda at: at - (1 - core) * count)
    total = dot(first_ref[...], own_place) + dot(more, more_place)

    def source(at):
        t, j = at // PIECE, at % PIECE
        return (t % N_Y * 2 + t // N_Y) * PIECE + j

    total = dot(one_hot(FEAT, FEAT, source), total.astype(jnp.bfloat16))
    for y in range(N_Y):
        pair = total[y * PAIR : (y + 1) * PAIR].astype(jnp.bfloat16)
        out_ref[y] = pair
        out_ref[N_Y + y] = pair


def project(heads, more_heads, w_ot):
    cost = pl.CostEstimate(
        flops=2 * FEAT * HALF * TOKENS, bytes_accessed=2 * 2**20, transcendentals=0
    )
    first = pl.pallas_call(
        project_own_kernel,
        out_shape=shape(FEAT, N_RING * NEW),
        in_specs=[VMEM] * 2,
        out_specs=VMEM,
        compiler_params=params(),
        cost_estimate=cost,
        name="project_own",
    )(heads, w_ot)
    return pl.pallas_call(
        project_more_kernel,
        out_shape=shape(N_TP, PAIR, TOKENS),
        in_specs=[VMEM] * 3,
        out_specs=VMEM,
        compiler_params=params(),
        cost_estimate=cost,
        name="project_more",
    )(first, more_heads, w_ot)


def update_kernel(parts_ref, residual_ref, updated_ref, out_ref):
    attended = jnp.sum(parts_ref[...].astype(jnp.float32), axis=0)
    updated = (dot(residual_ref[...], token_order()) + attended).astype(jnp.bfloat16)
    updated_ref[...] = updated
    for i in range(N_RING):
        out_ref[i] = updated


def update(parts, residual):
    return pl.pallas_call(
        update_kernel,
        out_shape=(shape(PAIR, TOKENS), shape(N_RING, PAIR, TOKENS)),
        in_specs=[VMEM] * 2,
        out_specs=(VMEM, VMEM),
        compiler_params=params(),
        name="update",
    )(parts, residual)


def spaced(ref):
    wide = ref[...].astype(jnp.float32).reshape(SIDE, TOKENS)
    squares = jnp.sum(wide * wide, axis=0, keepdims=True)
    wide = jnp.concatenate([wide, jnp.zeros((8, TOKENS), jnp.float32)], axis=0)
    pieces = [wide[i * PIECE : i * PIECE + PAD] for i in range(SIDE // PIECE)]
    return jnp.concatenate(pieces, axis=0).astype(jnp.bfloat16), squares


def mix_own_kernel(own_ref, *refs):
    blocks, (out_ref, squares_ref, held, sems) = refs[:N_Y], refs[N_Y:]
    copies = [
        pltpu.make_async_copy(blocks[k].at[:, pl.ds(0, OUT)], held.at[k], sems.at[k])
        for k in range(N_Y)
    ]
    for copy in copies:
        copy.start()
    own, squares_ref[...] = spaced(own_ref)
    for k in range(N_Y):
        copies[k].wait()
        out_ref[k] = dot(held[k], own)


def mix_more_kernel(part_ref, squares_ref, more_ref, *refs):
    blocks, (out_ref, held, sems) = refs[:N_Y], refs[N_Y:]
    copies = [
        pltpu.make_async_copy(blocks[k].at[:, pl.ds(OUT, OUT)], held.at[k], sems.at[k])
        for k in range(N_Y)
    ]
    for copy in copies:
        copy.start()
    more, squares = spaced(more_ref)
    squares = squares_ref[...] + squares
    high = squares.astype(jnp.bfloat16).astype(jnp.float32)
    row = lax.broadcasted_iota(jnp.int32, (16, TOKENS), 0)
    tail = jnp.where(row == 0, high, jnp.where(row == 1, squares - high, 0.0))
    tail = tail.astype(jnp.bfloat16)
    y = lax.axis_index("y")
    for k in range(N_Y):
        copies[k].wait()
        part = part_ref[k] + dot(held[k], more)
        out_ref[y ^ k, : 2 * FF, :] = part.astype(jnp.bfloat16)
        out_ref[y ^ k, 2 * FF :, :] = tail


def mix(own, more, blocks):
    scratch = [
        pltpu.VMEM((N_Y, 2 * FF, OUT), jnp.bfloat16),
        pltpu.SemaphoreType.DMA((N_Y,)),
    ]
    cost = pl.CostEstimate(
        flops=2 * N_Y * 2 * FF * OUT * TOKENS, bytes_accessed=4 * 2**20, transcendentals=0
    )
    part, squares = pl.pallas_call(
        mix_own_kernel,
        out_shape=(
            shape(N_Y, 2 * FF, TOKENS, dtype=jnp.float32),
            shape(1, TOKENS, dtype=jnp.float32),
        ),
        in_specs=[VMEM] + [ANY] * N_Y,
        out_specs=(VMEM, VMEM),
        scratch_shapes=scratch,
        compiler_params=params(),
        cost_estimate=cost,
        name="mix_own",
    )(own, *blocks)
    return pl.pallas_call(
        mix_more_kernel,
        out_shape=shape(N_Y, 2 * FF + 16, TOKENS),
        in_specs=[VMEM] * 3 + [ANY] * N_Y,
        out_specs=VMEM,
        scratch_shapes=scratch,
        compiler_params=params(),
        cost_estimate=cost,
        name="mix_more",
    )(part, squares, more, *blocks)


def gate_kernel(parts_ref, out_ref):
    total = jnp.sum(parts_ref[...].astype(jnp.float32), axis=0)
    mean = (total[2 * FF : 2 * FF + 1] + total[2 * FF + 1 : 2 * FF + 2]) * (1.0 / D)
    inverse_rms = lax.rsqrt(mean + EPS)
    gate_out, up_out = total[:FF] * inverse_rms, total[FF : 2 * FF] * inverse_rms
    hidden = gate_out / (1.0 + jnp.exp(-gate_out)) * up_out
    hidden = jnp.concatenate([hidden, jnp.zeros((ROOM - FF, TOKENS), jnp.float32)], axis=0)
    hidden = hidden.astype(jnp.bfloat16)
    for t in range(N_Y):
        out_ref[t] = hidden


def gate(parts):
    return pl.pallas_call(
        gate_kernel,
        out_shape=shape(N_Y, ROOM, TOKENS),
        in_specs=[VMEM],
        out_specs=VMEM,
        compiler_params=params(),
        name="gate",
    )(parts)


def down_kernel(side, hidden_ref, *refs):
    blocks, (out_ref, held, hidden, sems) = refs[:N_Y], refs[N_Y:]
    copies = [
        pltpu.make_async_copy(
            blocks[k].at[:, pl.ds(side * OUT, OUT)], held.at[pl.ds(k * ROOM, ROOM), :], sems.at[k]
        )
        for k in range(N_Y)
    ]
    for copy in copies:
        copy.start()
    y = lax.axis_index("y")
    for k in range(N_Y):
        hidden[k * ROOM : (k + 1) * ROOM, :] = hidden_ref[y ^ k]
    for copy in copies:
        copy.wait()
    out_ref[...] = dot(held[...], hidden[...], TN).astype(out_ref.dtype)


def down(side, hidden, blocks):
    return pl.pallas_call(
        functools.partial(down_kernel, side),
        out_shape=shape(OUT, TOKENS, dtype=jnp.bfloat16 if side else jnp.float32),
        in_specs=[VMEM] + [ANY] * N_Y,
        out_specs=VMEM,
        scratch_shapes=[
            pltpu.VMEM((N_Y * ROOM, OUT), jnp.bfloat16),
            pltpu.VMEM((N_Y * ROOM, TOKENS), jnp.bfloat16),
            pltpu.SemaphoreType.DMA((N_Y,)),
        ],
        compiler_params=params(),
        cost_estimate=pl.CostEstimate(
            flops=2 * N_Y * ROOM * OUT * TOKENS, bytes_accessed=3 * 2**20, transcendentals=0
        ),
        name="down",
    )(hidden, *blocks)


def finish_kernel(updated_ref, parts_ref, out_ref):
    wide = updated_ref[...].astype(jnp.float32)
    own = jnp.where(lax.axis_index("xh") == 0, wide[:PIECE], wide[PIECE:])
    total = own + jnp.sum(parts_ref[...].astype(jnp.float32), axis=0)[:PIECE]
    out_ref[...] = dot(total.astype(jnp.bfloat16), token_order(), NT).astype(jnp.bfloat16)


def finish(updated, parts):
    return pl.pallas_call(
        finish_kernel,
        out_shape=shape(PIECE, TOKENS),
        in_specs=[VMEM] * 2,
        out_specs=VMEM,
        compiler_params=params(),
        name="finish",
    )(updated, parts)


def swap(x, axes):
    return lax.all_to_all(x, axes, 0, 0, tiled=True)


def other_core(x):
    return lax.ppermute(x, "c", [(0, 1), (1, 0)])


def other_half(x):
    return lax.ppermute(x, "xh", [(0, 1), (1, 0)])


def body(
    queries, new_latent, cache, cache_lengths, w_uv, w_o, residual, norm_gain, w_gate, w_up, w_down
):
    xh = lax.axis_index("xh")

    heads = attend(
        cache_lengths.T, queries.reshape(ROWS, KDIM), jnp.transpose(new_latent, (1, 0, 2)), cache.T,
        w_uv,
    )

    def exchange(block, k):
        return lax.ppermute(block, "y", [(i, i ^ k) for i in range(N_Y)])

    gain = norm_gain.reshape(D // 128, 128)
    sources = (w_gate.T, w_up.T)
    mix_1, mix_3 = regroup((1, 3), sources, gain, heads)
    mix_2, mix_0 = regroup((2, 0), sources, gain, mix_1)

    heads = swap(heads, RING).reshape(TOKENS, HALF)
    heads, mix_1, mix_3, mix_0 = lax.optimization_barrier(
        (heads, exchange(mix_1, 1), exchange(mix_3, 3), mix_0)
    )
    partial = project(heads, other_core(heads), w_o.T)

    partner = other_half(residual.T)
    residual = jnp.concatenate(
        [jnp.where(xh == 0, residual.T, partner), jnp.where(xh == 0, partner, residual.T)], axis=0
    )
    down_blocks = regroup((1, 3, 2, 0), (w_down,), gain, partial)
    parts, mix_2, *down_blocks = lax.optimization_barrier(
        (swap(partial, TP), exchange(mix_2, 2), *down_blocks)
    )
    updated, block = update(parts, residual)
    down_1, down_3, down_2, down_0 = down_blocks
    own, down_1, down_2, down_3 = lax.optimization_barrier(
        (swap(block, RING), exchange(down_1, 1), exchange(down_2, 2), exchange(down_3, 3))
    )
    mix_blocks, down_blocks = (mix_0, mix_1, mix_2, mix_3), (down_0, down_1, down_2, down_3)
    hidden = gate(swap(mix(own, other_core(own), mix_blocks), "y"))
    hidden = swap(hidden, "y")
    more = other_core(down(1, hidden, down_blocks))
    term = down(0, hidden, down_blocks) + more.astype(jnp.float32)
    term = swap(term.astype(jnp.bfloat16).reshape(2 * N_RING, PAD, TOKENS), RING + ("xh",))
    return finish(updated, term).T


def solution(mesh):
    parts = Mesh(mesh.devices.reshape(tuple(SIZES.values())), tuple(SIZES))
    everywhere = DP + TP
    return jax.shard_map(
        body,
        mesh=parts,
        in_specs=(
            P(DP, None, TP, None),
            P(DP, None, None),
            P(DP, None),
            P(),
            P(TP, None, None),
            P(TP, DP),
            P(None, everywhere),
            P(),
            P(None, everywhere),
            P(None, everywhere),
            P(everywhere, None),
        ),
        out_specs=P(None, everywhere),
        check_vma=False,
    )
```

```python
import functools

import jax
import jax.numpy as jnp
from jax import lax
from jax.experimental import pallas as pl
from jax.experimental.pallas import tpu as pltpu
from jax.sharding import Mesh, PartitionSpec as P

DP = ("xl", "z", "c")
RING = ("xl", "z")
TP = ("xh", "y")
SIZES = {"xl": 2, "z": 8, "c": 2, "xh": 2, "y": 4}
N_RING, N_TP, N_Y = 16, 8, 4

STEPS, HEADS, REQ = 3, 16, 4
NEW = REQ * STEPS
ROWS = NEW * HEADS
TOKENS = 384
LAT, KDIM, VDIM = 512, 576, 128
HALF = HEADS // 2 * VDIM
CTX, CHUNK = 4096, 1024
N_CHUNK = CTX // CHUNK
D, FEAT, PIECE, PAD = 7168, 224, 28, 32
PAIR = 2 * PIECE
SIDE = N_RING * PAIR
OUT = N_RING * 2 * PAD
FF, ROOM = 72, 80
EPS = 1e-06
LOG2E = 1.4426950408889634
SCALE = 192.0 ** (-0.5)
NEG = -1e30

NT = (((1,), (1,)), ((), ()))
TN = (((0,), (0,)), ((), ()))

VMEM = pl.BlockSpec(memory_space=pltpu.VMEM)
SMEM = pl.BlockSpec(memory_space=pltpu.SMEM)
ANY = pl.BlockSpec(memory_space=pl.ANY)
HBM = pl.BlockSpec(memory_space=pltpu.HBM)


def params(mib=12):
    return pltpu.CompilerParams(vmem_limit_bytes=mib * 2**20)


def shape(*dims, dtype=jnp.bfloat16):
    return jax.ShapeDtypeStruct(dims, dtype)


def dot(a, b, dims=(((1,), (0,)), ((), ()))):
    return lax.dot_general(a, b, dims, preferred_element_type=jnp.float32)


def attend_kernel(
    lengths, q_ref, fresh_ref, cache_hbm, w_uv_hbm, out_ref, keys, scores, w_uv,
    new_keys, key_sems, w_sem,
):
    copies = [
        pltpu.make_async_copy(
            cache_hbm.at[:, pl.ds(j * CHUNK, CHUNK)], keys.at[j], key_sems.at[j]
        )
        for j in range(N_CHUNK)
    ]
    w_copy = pltpu.make_async_copy(w_uv_hbm, w_uv, w_sem)
    for copy in copies:
        copy.start()

    dp_index = lax.axis_index(DP)
    q = q_ref[...]
    row = lax.broadcasted_iota(jnp.int32, (ROWS, 1), 0)
    request = row // (STEPS * HEADS)
    step = row // HEADS - request * STEPS
    low = jnp.zeros((ROWS, 1), jnp.int32)
    high = jnp.zeros((ROWS, 1), jnp.int32)
    start = 0
    for r in range(REQ):
        end = start + lengths[r, dp_index]
        low = jnp.where(request == r, start, low)
        high = jnp.where(request == r, end, high)
        start = end

    new_keys[...] = jnp.zeros_like(new_keys)
    for i in range(STEPS):
        new_keys[i * REQ : (i + 1) * REQ, :] = fresh_ref[i].astype(jnp.float32)
    fresh = new_keys[...].astype(jnp.bfloat16)
    key = lax.broadcasted_iota(jnp.int32, (ROWS, 16), 1)
    key_step = key // REQ
    seen = (key - key_step * REQ == request) & (key_step <= step)
    fresh_scores = jnp.where(seen, dot(q, fresh, NT) * (SCALE * LOG2E), NEG)
    top = jnp.max(fresh_scores, axis=1, keepdims=True)

    tops = jnp.full((ROWS, 128), NEG, jnp.float32)
    for j in range(N_CHUNK):
        copies[j].wait()
        if j == 1:
            w_copy.start()
        slot = j * CHUNK + lax.broadcasted_iota(jnp.int32, (ROWS, CHUNK), 1)
        part = dot(q, keys[j]) * (SCALE * LOG2E)
        part = jnp.where((slot >= low) & (slot < high), part, NEG)
        scores[j] = part
        for i in range(0, CHUNK, 128):
            tops = jnp.maximum(tops, part[:, i : i + 128])
    top = jnp.maximum(top, jnp.max(tops, axis=1, keepdims=True))

    totals = jnp.zeros((ROWS, 128), jnp.float32)
    weights = jnp.exp2(fresh_scores - top)
    total = jnp.sum(weights, axis=1, keepdims=True)
    mixed = dot(weights.astype(jnp.bfloat16), fresh[:, :LAT])
    for j in range(N_CHUNK):
        weights = jnp.exp2(scores[j] - top)
        for i in range(0, CHUNK, 128):
            totals = totals + weights[:, i : i + 128]
        mixed = mixed + dot(weights.astype(jnp.bfloat16), keys[j, :LAT, :], NT)
    total = total + jnp.sum(totals, axis=1, keepdims=True)
    mixed = (mixed / total).astype(jnp.bfloat16)

    w_copy.wait()
    head = row - (row // HEADS) * HEADS
    halves = []
    for half in range(2):
        values = []
        for h in range(half * HEADS // 2, (half + 1) * HEADS // 2, 2):
            pair = dot(mixed, jnp.concatenate([w_uv[h], w_uv[h + 1]], axis=1))
            for i in range(2):
                value = jnp.where(head == h + i, pair[:, i * VDIM : (i + 1) * VDIM], 0.0)
                values.append(jnp.sum(value.reshape(NEW, HEADS, VDIM), axis=1))
        halves.append(jnp.concatenate(values, axis=1))
    both = jnp.concatenate(halves, axis=0).astype(jnp.bfloat16)
    for i in range(N_RING):
        out_ref[i] = both


def attend(lengths, q, fresh, cache_t, w_uv):
    return pl.pallas_call(
        attend_kernel,
        out_shape=shape(N_RING, 2 * NEW, HALF),
        in_specs=[SMEM, VMEM, VMEM, ANY, ANY],
        out_specs=VMEM,
        scratch_shapes=[
            pltpu.VMEM((N_CHUNK, KDIM, CHUNK), jnp.bfloat16),
            pltpu.VMEM((N_CHUNK, ROWS, CHUNK), jnp.float32),
            pltpu.VMEM((HEADS, LAT, VDIM), jnp.bfloat16),
            pltpu.VMEM((16, KDIM), jnp.float32),
            pltpu.SemaphoreType.DMA((N_CHUNK,)),
            pltpu.SemaphoreType.DMA,
        ],
        compiler_params=params(58),
        cost_estimate=pl.CostEstimate(
            flops=2 * ROWS * CTX * (KDIM + LAT), bytes_accessed=7 * 2**20, transcendentals=ROWS * CTX
        ),
        name="attend",
    )(lengths, q, fresh, cache_t, w_uv)


def one_hot(rows, columns, source):
    column = lax.broadcasted_iota(jnp.int32, (1, columns), 1)
    row = lax.broadcasted_iota(jnp.int32, (rows, columns), 0)
    return jnp.where(row == source(column), 1.0, 0.0).astype(jnp.bfloat16)


def token_order():
    def source(at):
        core, rest = at // (N_RING * NEW), at % (N_RING * NEW)
        return (rest // NEW * 2 + core) * NEW + rest % NEW

    return one_hot(TOKENS, TOKENS, source)


def pick_columns(ks, width):
    lanes = len(ks) * 8 * PAD
    lane = lax.broadcasted_iota(jnp.int32, (1, lanes), 1)
    n, side, u = lane // (8 * PAD), lane // (4 * PAD) % 2, lane // (2 * PAD) % 2
    k = jnp.zeros_like(n)
    for i in range(len(ks)):
        k = jnp.where(n == i, ks[i], k)
    xh, j = lane // PAD % 2, lane % PAD
    source = (2 * u + (side ^ lax.axis_index("c"))) * FEAT
    source = source + (xh * N_Y + (k ^ lax.axis_index("y"))) * PIECE + j
    source = jnp.where(j < PIECE, source, -1)
    rows = lax.broadcasted_iota(jnp.int32, (width, lanes), 0)
    return jnp.where(rows == source, 1.0, 0.0).astype(jnp.bfloat16)


def regroup_kernel(ks, count, *refs):
    sources, gain_ref, refs = refs[:count], refs[count], refs[count + 2 :]
    outs, (rows, moved_ref, out_sems) = refs[:-3], refs[-3:]
    width = 4 * FEAT
    pick = pick_columns(ks, width)
    for j in range(D // 128):
        lanes = slice(j * 128, (j + 1) * 128)
        wide = [ref[:, lanes].astype(jnp.float32) for ref in sources]
        if count == 2:
            wide = jnp.concatenate(wide, axis=0) * gain_ref[j : j + 1, :].astype(jnp.float32)
        else:
            wide = jnp.concatenate(wide + [jnp.zeros((ROOM - FF, 128), jnp.float32)], axis=0)
        rows[:, lanes] = wide.astype(jnp.bfloat16)
    stores = []
    for n in range(len(ks)):
        for m in range(D // width):
            moved = dot(rows[:, m * width : (m + 1) * width], pick[:, n * 256 : (n + 1) * 256])
            moved = moved.astype(jnp.bfloat16)
            for side in range(2):
                to = (side * 8 + m) * 128
                moved_ref[n, :, to : to + 128] = moved[:, side * 128 : (side + 1) * 128]
        stores.append(pltpu.make_async_copy(moved_ref.at[n], outs[n], out_sems.at[n]))
        stores[-1].start()
    for store in stores:
        store.wait()


def regroup(ks, sources, gain, after):
    count = len(sources)
    height = 2 * FF if count == 2 else ROOM
    return pl.pallas_call(
        functools.partial(regroup_kernel, ks, count),
        out_shape=[shape(height, 2 * OUT)] * len(ks),
        in_specs=[VMEM] * (count + 1) + [ANY],
        out_specs=[HBM] * len(ks),
        scratch_shapes=[
            pltpu.VMEM((height, D), jnp.bfloat16),
            pltpu.VMEM((len(ks), height, 2 * OUT), jnp.bfloat16),
            pltpu.SemaphoreType.DMA((len(ks),)),
        ],
        compiler_params=params(58),
        cost_estimate=pl.CostEstimate(
            flops=2 * height * D * 256 * len(ks), bytes_accessed=5 * 2**20, transcendentals=0
        ),
        name="regroup",
    )(*sources, gain, after)


def project_heads(heads_ref, w_ref):
    def source(at):
        ring, rest = at // (2 * NEW), at % (2 * NEW)
        return rest // NEW * (N_RING * NEW) + ring * NEW + rest % NEW

    split = one_hot(TOKENS, TOKENS, source)
    heads = dot(split, heads_ref[...]).astype(jnp.bfloat16)
    return dot(w_ref[:, :HALF], heads[: N_RING * NEW], NT) + dot(
        w_ref[:, HALF:], heads[N_RING * NEW :], NT
    )


def project_own_kernel(heads_ref, w_ref, out_ref):
    out_ref[...] = project_heads(heads_ref, w_ref).astype(jnp.bfloat16)


def project_more_kernel(first_ref, heads_ref, w_ref, out_ref):
    more = project_heads(heads_ref, w_ref).astype(jnp.bfloat16)
    core, count = lax.axis_index("c"), N_RING * NEW
    own_place = one_hot(count, TOKENS, lambda at: at - core * count)
    more_place = one_hot(count, TOKENS, lambda at: at - (1 - core) * count)
    total = dot(first_ref[...], own_place) + dot(more, more_place)

    def source(at):
        t, j = at // PIECE, at % PIECE
        return (t % N_Y * 2 + t // N_Y) * PIECE + j

    total = dot(one_hot(FEAT, FEAT, source), total.astype(jnp.bfloat16))
    for y in range(N_Y):
        pair = total[y * PAIR : (y + 1) * PAIR].astype(jnp.bfloat16)
        out_ref[y] = pair
        out_ref[N_Y + y] = pair


def project(heads, more_heads, w_ot):
    cost = pl.CostEstimate(
        flops=2 * FEAT * HALF * TOKENS, bytes_accessed=2 * 2**20, transcendentals=0
    )
    first = pl.pallas_call(
        project_own_kernel,
        out_shape=shape(FEAT, N_RING * NEW),
        in_specs=[VMEM] * 2,
        out_specs=VMEM,
        compiler_params=params(),
        cost_estimate=cost,
        name="project_own",
    )(heads, w_ot)
    return pl.pallas_call(
        project_more_kernel,
        out_shape=shape(N_TP, PAIR, TOKENS),
        in_specs=[VMEM] * 3,
        out_specs=VMEM,
        compiler_params=params(),
        cost_estimate=cost,
        name="project_more",
    )(first, more_heads, w_ot)


def update_kernel(parts_ref, residual_ref, updated_ref, out_ref):
    attended = jnp.sum(parts_ref[...].astype(jnp.float32), axis=0)
    updated = (dot(residual_ref[...], token_order()) + attended).astype(jnp.bfloat16)
    updated_ref[...] = updated
    for i in range(N_RING):
        out_ref[i] = updated


def update(parts, residual):
    return pl.pallas_call(
        update_kernel,
        out_shape=(shape(PAIR, TOKENS), shape(N_RING, PAIR, TOKENS)),
        in_specs=[VMEM] * 2,
        out_specs=(VMEM, VMEM),
        compiler_params=params(),
        name="update",
    )(parts, residual)


def spaced(ref):
    wide = ref[...].astype(jnp.float32).reshape(SIDE, TOKENS)
    squares = jnp.sum(wide * wide, axis=0, keepdims=True)
    wide = jnp.concatenate([wide, jnp.zeros((8, TOKENS), jnp.float32)], axis=0)
    pieces = [wide[i * PIECE : i * PIECE + PAD] for i in range(SIDE // PIECE)]
    return jnp.concatenate(pieces, axis=0).astype(jnp.bfloat16), squares


def mix_own_kernel(own_ref, *refs):
    blocks, (out_ref, squares_ref) = refs[:N_Y], refs[N_Y:]
    own, squares_ref[...] = spaced(own_ref)
    for k in range(N_Y):
        out_ref[k] = dot(blocks[k][:, :OUT], own)


def mix_more_kernel(part_ref, squares_ref, more_ref, *refs):
    blocks, out_ref = refs[:N_Y], refs[N_Y]
    more, squares = spaced(more_ref)
    squares = squares_ref[...] + squares
    high = squares.astype(jnp.bfloat16).astype(jnp.float32)
    row = lax.broadcasted_iota(jnp.int32, (16, TOKENS), 0)
    tail = jnp.where(row == 0, high, jnp.where(row == 1, squares - high, 0.0))
    tail = tail.astype(jnp.bfloat16)
    y = lax.axis_index("y")
    for k in range(N_Y):
        part = part_ref[k] + dot(blocks[k][:, OUT:], more)
        out_ref[y ^ k, : 2 * FF, :] = part.astype(jnp.bfloat16)
        out_ref[y ^ k, 2 * FF :, :] = tail


def mix(own, more, blocks):
    cost = pl.CostEstimate(
        flops=2 * N_Y * 2 * FF * OUT * TOKENS, bytes_accessed=4 * 2**20, transcendentals=0
    )
    part, squares = pl.pallas_call(
        mix_own_kernel,
        out_shape=(
            shape(N_Y, 2 * FF, TOKENS, dtype=jnp.float32),
            shape(1, TOKENS, dtype=jnp.float32),
        ),
        in_specs=[VMEM] * (1 + N_Y),
        out_specs=(VMEM, VMEM),
        compiler_params=params(16),
        cost_estimate=cost,
        name="mix_own",
    )(own, *blocks)
    return pl.pallas_call(
        mix_more_kernel,
        out_shape=shape(N_Y, 2 * FF + 16, TOKENS),
        in_specs=[VMEM] * (3 + N_Y),
        out_specs=VMEM,
        compiler_params=params(16),
        cost_estimate=cost,
        name="mix_more",
    )(part, squares, more, *blocks)


def gate_kernel(parts_ref, out_ref):
    total = jnp.sum(parts_ref[...].astype(jnp.float32), axis=0)
    mean = (total[2 * FF : 2 * FF + 1] + total[2 * FF + 1 : 2 * FF + 2]) * (1.0 / D)
    inverse_rms = lax.rsqrt(mean + EPS)
    gate_out, up_out = total[:FF] * inverse_rms, total[FF : 2 * FF] * inverse_rms
    hidden = gate_out / (1.0 + jnp.exp(-gate_out)) * up_out
    hidden = jnp.concatenate([hidden, jnp.zeros((ROOM - FF, TOKENS), jnp.float32)], axis=0)
    hidden = hidden.astype(jnp.bfloat16)
    for t in range(N_Y):
        out_ref[t] = hidden


def gate(parts):
    return pl.pallas_call(
        gate_kernel,
        out_shape=shape(N_Y, ROOM, TOKENS),
        in_specs=[VMEM],
        out_specs=VMEM,
        compiler_params=params(),
        name="gate",
    )(parts)


def down_kernel(side, hidden_ref, *refs):
    blocks, (out_ref, held, hidden, sems) = refs[:N_Y], refs[N_Y:]
    copies = [
        pltpu.make_async_copy(
            blocks[k].at[:, pl.ds(side * OUT, OUT)], held.at[pl.ds(k * ROOM, ROOM), :], sems.at[k]
        )
        for k in range(N_Y)
    ]
    for copy in copies:
        copy.start()
    y = lax.axis_index("y")
    for k in range(N_Y):
        hidden[k * ROOM : (k + 1) * ROOM, :] = hidden_ref[y ^ k]
    for copy in copies:
        copy.wait()
    out_ref[...] = dot(held[...], hidden[...], TN).astype(out_ref.dtype)


def down(side, hidden, blocks):
    return pl.pallas_call(
        functools.partial(down_kernel, side),
        out_shape=shape(OUT, TOKENS, dtype=jnp.bfloat16 if side else jnp.float32),
        in_specs=[VMEM] + [ANY] * N_Y,
        out_specs=VMEM,
        scratch_shapes=[
            pltpu.VMEM((N_Y * ROOM, OUT), jnp.bfloat16),
            pltpu.VMEM((N_Y * ROOM, TOKENS), jnp.bfloat16),
            pltpu.SemaphoreType.DMA((N_Y,)),
        ],
        compiler_params=params(),
        cost_estimate=pl.CostEstimate(
            flops=2 * N_Y * ROOM * OUT * TOKENS, bytes_accessed=3 * 2**20, transcendentals=0
        ),
        name="down",
    )(hidden, *blocks)


def finish_kernel(updated_ref, parts_ref, out_ref):
    wide = updated_ref[...].astype(jnp.float32)
    own = jnp.where(lax.axis_index("xh") == 0, wide[:PIECE], wide[PIECE:])
    total = own + jnp.sum(parts_ref[...].astype(jnp.float32), axis=0)[:PIECE]
    out_ref[...] = dot(total.astype(jnp.bfloat16), token_order(), NT).astype(jnp.bfloat16)


def finish(updated, parts):
    return pl.pallas_call(
        finish_kernel,
        out_shape=shape(PIECE, TOKENS),
        in_specs=[VMEM] * 2,
        out_specs=VMEM,
        compiler_params=params(),
        name="finish",
    )(updated, parts)


def swap(x, axes):
    return lax.all_to_all(x, axes, 0, 0, tiled=True)


def other_core(x):
    return lax.ppermute(x, "c", [(0, 1), (1, 0)])


def other_half(x):
    return lax.ppermute(x, "xh", [(0, 1), (1, 0)])


def body(
    queries, new_latent, cache, cache_lengths, w_uv, w_o, residual, norm_gain, w_gate, w_up, w_down
):
    xh = lax.axis_index("xh")

    heads = attend(
        cache_lengths.T, queries.reshape(ROWS, KDIM), jnp.transpose(new_latent, (1, 0, 2)), cache.T,
        w_uv,
    )

    def exchange(block, k):
        return lax.ppermute(block, "y", [(i, i ^ k) for i in range(N_Y)])

    gain = norm_gain.reshape(D // 128, 128)
    sources = (w_gate.T, w_up.T)
    mix_1, mix_3 = regroup((1, 3), sources, gain, heads)
    mix_2, mix_0 = regroup((2, 0), sources, gain, mix_1)

    heads = swap(heads, RING).reshape(TOKENS, HALF)
    heads, mix_1, mix_3, mix_0 = lax.optimization_barrier(
        (heads, exchange(mix_1, 1), exchange(mix_3, 3), mix_0)
    )
    partial = project(heads, other_core(heads), w_o.T)

    partner = other_half(residual.T)
    residual = jnp.concatenate(
        [jnp.where(xh == 0, residual.T, partner), jnp.where(xh == 0, partner, residual.T)], axis=0
    )
    down_blocks = regroup((1, 3, 2, 0), (w_down,), gain, partial)
    parts, mix_2, *down_blocks = lax.optimization_barrier(
        (swap(partial, TP), exchange(mix_2, 2), *down_blocks)
    )
    updated, block = update(parts, residual)
    down_1, down_3, down_2, down_0 = down_blocks
    own, down_1, down_2, down_3 = lax.optimization_barrier(
        (swap(block, RING), exchange(down_1, 1), exchange(down_2, 2), exchange(down_3, 3))
    )
    mix_blocks, down_blocks = (mix_0, mix_1, mix_2, mix_3), (down_0, down_1, down_2, down_3)
    hidden = gate(swap(mix(own, other_core(own), mix_blocks), "y"))
    hidden = swap(hidden, "y")
    more = other_core(down(1, hidden, down_blocks))
    term = down(0, hidden, down_blocks) + more.astype(jnp.float32)
    term = swap(term.astype(jnp.bfloat16).reshape(2 * N_RING, PAD, TOKENS), RING + ("xh",))
    return finish(updated, term).T


def solution(mesh):
    parts = Mesh(mesh.devices.reshape(tuple(SIZES.values())), tuple(SIZES))
    everywhere = DP + TP
    return jax.shard_map(
        body,
        mesh=parts,
        in_specs=(
            P(DP, None, TP, None),
            P(DP, None, None),
            P(DP, None),
            P(),
            P(TP, None, None),
            P(TP, DP),
            P(None, everywhere),
            P(),
            P(None, everywhere),
            P(None, everywhere),
            P(everywhere, None),
        ),
        out_specs=P(None, everywhere),
        check_vma=False,
    )
```
